32 devices in a mesh: clip: 8 (over z, x), band: 4 (over y, core).
Axes of the slice: x: 2, y: 2, z: 4, core: 2. Of those that a mesh axis runs over, the one named last changes fastest.
Arguments:
- tokens: bfloat16 [8, 3072, 1024], P('clip', 'band'), may hold values from -6 to 6
- cotangent: bfloat16 [8, 3072, 1024], P('clip', 'band'), may hold values from -6 to 6
- frame_counts: int32 [8], P('clip'), may hold values from 6 to 12, as said below
- noise_levels: int32 [8, 12], P('clip'), may hold values from 0 to 999
- qkv_master: float32 [1024, 3072], P(('clip', 'band')), may hold values from -0.25 to 0.25
- out_master: float32 [1024, 1024], P(('clip', 'band')), may hold values from -0.375 to 0.375
- up_master: float32 [1024, 4096], P(('clip', 'band')), may hold values from -0.1875 to 0.1875
- down_master: float32 [4096, 1024], P(('clip', 'band')), may hold values from -0.09375 to 0.09375
- ada_master: float32 [1024, 6144], P(('clip', 'band')), may hold values from -0.1875 to 0.1875
- qkv_first: float32 [1024, 3072], P(('clip', 'band')), may hold values from -0.00036621094 to 0.00036621094
- out_first: float32 [1024, 1024], P(('clip', 'band')), may hold values from -0.00036621094 to 0.00036621094
- up_first: float32 [1024, 4096], P(('clip', 'band')), may hold values from -0.00036621094 to 0.00036621094
- down_first: float32 [4096, 1024], P(('clip', 'band')), may hold values from -0.00036621094 to 0.00036621094
- ada_first: float32 [1024, 6144], P(('clip', 'band')), may hold values from -0.00036621094 to 0.00036621094
- qkv_second: float32 [1024, 3072], P(('clip', 'band')), may hold values from 5.3511723e-10 to 2.140469e-09
- out_second: float32 [1024, 1024], P(('clip', 'band')), may hold values from 5.3511723e-10 to 2.140469e-09
- up_second: float32 [1024, 4096], P(('clip', 'band')), may hold values from 5.3511723e-10 to 2.140469e-09
- down_second: float32 [4096, 1024], P(('clip', 'band')), may hold values from 5.3511723e-10 to 2.140469e-09
- ada_second: float32 [1024, 6144], P(('clip', 'band')), may hold values from 5.3511723e-10 to 2.140469e-09
Outputs:
- activations: bfloat16 [8, 3072, 1024], P('clip', 'band')
- input_grad: float32 [8, 3072, 1024], P('clip', 'band')
- grad_norm: float32 [], replicated
- qkv_updated: float32 [1024, 3072], P(('clip', 'band'))
- qkv_first_new: float32 [1024, 3072], P(('clip', 'band'))
- qkv_second_new: float32 [1024, 3072], P(('clip', 'band'))
- out_updated: float32 [1024, 1024], P(('clip', 'band'))
- out_first_new: float32 [1024, 1024], P(('clip', 'band'))
- out_second_new: float32 [1024, 1024], P(('clip', 'band'))
- up_updated: float32 [1024, 4096], P(('clip', 'band'))
- up_first_new: float32 [1024, 4096], P(('clip', 'band'))
- up_second_new: float32 [1024, 4096], P(('clip', 'band'))
- down_updated: float32 [4096, 1024], P(('clip', 'band'))
- down_first_new: float32 [4096, 1024], P(('clip', 'band'))
- down_second_new: float32 [4096, 1024], P(('clip', 'band'))
- ada_updated: float32 [1024, 6144], P(('clip', 'band'))
- ada_first_new: float32 [1024, 6144], P(('clip', 'band'))
- ada_second_new: float32 [1024, 6144], P(('clip', 'band'))
The draws below stay inside these ranges and needn't reach their ends.
Inputs may be any that keep to these rules, and one draw needn't show every extreme that they name: `frame_counts`: frames at or after a clip's count are padding and are never attended to as keys; some clip holds 12 frames and some other clip 12 // 2.
All inputs are finite; a program needn't handle non-finite values.
Results may differ from the reference program's by a relative error of at most 0.014.
The reference program's roundings to bfloat16 on the way count: a program that leaves them out, or rounds other values in their place, can miss the bound.
Values may be sent and summed in bfloat16 or wider, within the bound.
No kernel may reach another device: no remote copies, remote signals or barrier semaphores. Data moves between devices by JAX's collectives and lax.ppermute only.
A program may use at most 256 MiB of HBM per device.

```python
import math
import jax
import jax.numpy as jnp
from jax import lax

D = 1024
HEADS = 16
HEAD_DIM = 64
FF = 4096
FRAMES = 12
COLS = 16
LEVELS = 1000
STEP = 10
CLIPS = 8
BAND_ROWS = 4
LOCAL = 768
CLIP_TOKENS = 3072


def draw_frame_counts(key, part):
    key = jax.random.fold_in(key, 11)
    first_key, second_key, third_key = jax.random.split(key, 3)
    counts = jax.random.randint(first_key, (CLIPS,), FRAMES // 2, FRAMES + 1)
    longest = jax.random.randint(second_key, (), 0, CLIPS)
    shortest = (longest + jax.random.randint(third_key, (), 1, CLIPS)) % CLIPS
    counts = counts.at[longest].set(FRAMES).at[shortest].set(FRAMES // 2)
    return counts.astype(jnp.int32)


def with_ends(entries, stream_key, least, largest):
    index_at = [jax.random.randint(jax.random.fold_in(stream_key, axis), (), 0, length) for axis, length in enumerate(entries.shape)]
    widest = entries.shape.index(max(entries.shape))
    neighbour = index_at[:widest] + [(index_at[widest] + 1) % entries.shape[widest]] + index_at[widest + 1:]
    return entries.at[tuple(index_at)].set(least).at[tuple(neighbour)].set(largest)


def block_levels(own_key, dims, cuts, low, high):
    def one(dim, parts):
        heights = jax.random.uniform(jax.random.fold_in(jax.random.fold_in(own_key, 6), dim), (parts,), jnp.float32, low / len(cuts), high / len(cuts))
        return jnp.repeat(jnp.exp(heights), dims[dim] // parts).reshape((-1,) + (1,) * (len(dims) - dim - 1))

    level = one(*cuts[0])
    for cut in cuts[1:]:
        level = level * one(*cut)
    return level


def noise(key, shape, spread, most, cuts=(), held_as=jnp.bfloat16):
    factor_of = block_levels(key, shape, cuts, -0.22, 0.18) if cuts else 1.0
    entries = jax.random.normal(key, shape, jnp.float32) * spread * factor_of
    return jnp.minimum(jnp.maximum(entries, -most), most).astype(held_as)


def setup_inputs(seed: int = 0) -> dict:
    key_list = jax.random.split(jax.random.key(seed), 20)
    return {
        "tokens": noise(key_list[0], (CLIPS, CLIP_TOKENS, D), 1.0, 6.0, ((0, 8), (1, 4))),
        "cotangent": noise(key_list[1], (CLIPS, CLIP_TOKENS, D), 1.0, 6.0, ((0, 8), (1, 4))),
        "frame_counts": draw_frame_counts(jax.random.fold_in(key_list[19], 71), 0),
        "noise_levels": with_ends(jax.random.randint(key_list[3], (CLIPS, FRAMES), 0, LEVELS), jax.random.fold_in(key_list[3], 1), 0, LEVELS - 1).astype(jnp.int32),
        "qkv_master": noise(key_list[4], (D, 3 * D), (D // 2) ** -0.5, 0.25, ((0, 32),), jnp.float32),
        "out_master": noise(key_list[5], (D, D), (D // 4) ** -0.5, 0.375, ((0, 32),), jnp.float32),
        "up_master": noise(key_list[6], (D, FF), D ** -0.5, 0.1875, ((0, 32),), jnp.float32),
        "down_master": noise(key_list[7], (FF, D), FF ** -0.5, 0.09375, ((0, 32),), jnp.float32),
        "ada_master": noise(key_list[8], (D, 6 * D), D ** -0.5, 0.1875, ((0, 32),), jnp.float32),
        "qkv_first": noise(key_list[9], (D, 3 * D), (0.111 * (10 * D * D + 2 * D * FF) ** -0.5), 0.00036621094, ((0, 32),), jnp.float32),
        "out_first": noise(key_list[10], (D, D), (0.111 * (10 * D * D + 2 * D * FF) ** -0.5), 0.00036621094, ((0, 32),), jnp.float32),
        "up_first": noise(key_list[11], (D, FF), (0.111 * (10 * D * D + 2 * D * FF) ** -0.5), 0.00036621094, ((0, 32),), jnp.float32),
        "down_first": noise(key_list[12], (FF, D), (0.111 * (10 * D * D + 2 * D * FF) ** -0.5), 0.00036621094, ((0, 32),), jnp.float32),
        "ada_first": noise(key_list[13], (D, 6 * D), (0.111 * (10 * D * D + 2 * D * FF) ** -0.5), 0.00036621094, ((0, 32),), jnp.float32),
        "qkv_second": jnp.clip(jnp.exp(math.log(2.1404689132253907e-09) - 1.3862944 * jax.random.uniform(key_list[14], (D, 3 * D), jnp.float32) ** block_levels(key_list[14], (D, 3 * D), ((0, 32),), -0.2, 0.2)), 5.351172283063477e-10, 2.1404689132253907e-09),
        "out_second": jnp.clip(jnp.exp(math.log(2.1404689132253907e-09) - 1.3862944 * jax.random.uniform(key_list[15], (D, D), jnp.float32) ** block_levels(key_list[15], (D, D), ((0, 32),), -0.2, 0.2)), 5.351172283063477e-10, 2.1404689132253907e-09),
        "up_second": jnp.clip(jnp.exp(math.log(2.1404689132253907e-09) - 1.3862944 * jax.random.uniform(key_list[16], (D, FF), jnp.float32) ** block_levels(key_list[16], (D, FF), ((0, 32),), -0.2, 0.2)), 5.351172283063477e-10, 2.1404689132253907e-09),
        "down_second": jnp.clip(jnp.exp(math.log(2.1404689132253907e-09) - 1.3862944 * jax.random.uniform(key_list[17], (FF, D), jnp.float32) ** block_levels(key_list[17], (FF, D), ((0, 32),), -0.2, 0.2)), 5.351172283063477e-10, 2.1404689132253907e-09),
        "ada_second": jnp.clip(jnp.exp(math.log(2.1404689132253907e-09) - 1.3862944 * jax.random.uniform(key_list[18], (D, 6 * D), jnp.float32) ** block_levels(key_list[18], (D, 6 * D), ((0, 32),), -0.2, 0.2)), 5.351172283063477e-10, 2.1404689132253907e-09),
    }


@jax.custom_vjp
def low(v):
    return lax.optimization_barrier(v.astype(jnp.bfloat16)).astype(jnp.float32)

@jax.custom_vjp
def low_back(v):
    return v

def low_keep(v):
    return (low(v), None)

def low_pass(kept, grad):
    return (grad,)

def back_keep(v):
    return (v, None)

def back_low(kept, grad):
    return (low(grad),)
low.defvjp(low_keep, low_pass)
low_back.defvjp(back_keep, back_low)
beta_first = 0.9
beta_second = 0.99
learn_rate = 0.03
weight_decay = 0.01
adam_epsilon = 1e-08
clip_limit = 1.0
norm_epsilon = 1e-06
masked_score = -1000000000.0

def product(left, right):
    return jnp.dot(left, right, precision=lax.Precision.HIGHEST, preferred_element_type=jnp.float32)

def normalize(values):
    average = lax.optimization_barrier(jnp.mean(values, axis=-1, keepdims=True))
    centred = values - average
    variance = lax.optimization_barrier(jnp.mean(centred * centred, axis=-1, keepdims=True))
    return centred * lax.rsqrt(variance + norm_epsilon)

def embed_levels(levels):
    halfway = D // 2
    spacing = jnp.exp(-math.log(10000.0) * jnp.arange(halfway, dtype=jnp.float32) / halfway)
    angles = levels.astype(jnp.float32)[..., None] * spacing
    return jax.nn.silu(jnp.concatenate([jnp.cos(angles), jnp.sin(angles)], axis=-1))

def attend_head(pieces, key_valid):
    query_head, key_head, value_head = pieces
    scores = low_back(product(query_head, key_head.T) * 0.125)
    scores = jnp.where(key_valid[None, :], scores, masked_score)
    probability = jax.nn.softmax(scores, axis=-1)
    return product(low(probability), value_head)

def split_heads(tensor):
    return tensor.reshape(CLIP_TOKENS, HEADS, HEAD_DIM).transpose(1, 0, 2)

def forward(residual, weights, condition, key_valid, frame_of):
    w_qkv, w_out, w_up, w_down, w_ada = weights
    modulation = product(condition, w_ada)[frame_of]
    shift_one, scale_one, gate_one, shift_two, scale_two, gate_two = jnp.split(modulation, 6, axis=1)
    first_in = low(normalize(residual) * (1.0 + scale_one) + shift_one)
    projected = product(first_in, w_qkv)
    query_array = low_back(low(projected[:, :D]))
    key_array = low_back(low(projected[:, D:2 * D]))
    value_array = low_back(low(projected[:, 2 * D:]))
    head_step = jax.checkpoint(lambda pieces: attend_head(pieces, key_valid))
    attended = lax.map(head_step, (split_heads(query_array), split_heads(key_array), split_heads(value_array)))
    attended = low_back(low(attended.transpose(1, 0, 2).reshape(CLIP_TOKENS, D)))
    branch_one = low_back(product(attended, w_out))
    middle = residual + gate_one * branch_one
    second_in = low(normalize(middle) * (1.0 + scale_two) + shift_two)
    pre_act = low_back(product(second_in, w_up))
    hidden = low(jax.nn.gelu(pre_act, approximate=True))
    branch_two = low_back(product(hidden, w_down))
    return middle + gate_two * branch_two

def adam_step(master, clipped, first, second):
    first_new = beta_first * first + (1.0 - beta_first) * clipped
    second_new = beta_second * second + (1.0 - beta_second) * clipped * clipped
    first_hat = first_new / (1.0 - beta_first ** STEP)
    second_hat = second_new / (1.0 - beta_second ** STEP)
    updated = master - learn_rate * (first_hat / (jnp.sqrt(second_hat) + adam_epsilon) + weight_decay * master)
    return (updated, first_new, second_new)

def reference(tokens, cotangent, frame_counts, noise_levels, qkv_master, out_master, up_master, down_master, ada_master, qkv_first, out_first, up_first, down_first, ada_first, qkv_second, out_second, up_second, down_second, ada_second):
    masters = (qkv_master, out_master, up_master, down_master, ada_master)
    weights = tuple((low(master) for master in masters))
    conditions = low(embed_levels(noise_levels))
    frame_of = (jnp.arange(CLIP_TOKENS, dtype=jnp.int32) % LOCAL // (BAND_ROWS * COLS)).astype(jnp.int32)

    def per_clip(running, clip_item):
        clip_tokens, clip_cotangent, clip_count, clip_condition = clip_item
        key_valid = frame_of < clip_count

        def run_layer(residual, *layer_weights):
            return forward(residual, layer_weights, clip_condition, key_valid, frame_of)
        result, pullback = jax.vjp(run_layer, clip_tokens.astype(jnp.float32), *weights)
        gradients = pullback(clip_cotangent.astype(jnp.float32))
        running = tuple((summed + gradient for summed, gradient in zip(running, gradients[1:])))
        return (running, (result.astype(jnp.bfloat16), gradients[0]))
    zero_sums = tuple((jnp.zeros(master.shape, jnp.float32) for master in masters))
    summed, (activations, input_grad) = lax.scan(per_clip, zero_sums, (tokens, cotangent, frame_counts, conditions))
    squares = jnp.float32(0.0)
    for gradient in summed:
        squares = squares + jnp.sum(gradient * gradient)
    grad_norm = jnp.sqrt(squares)
    factor = jnp.minimum(1.0, clip_limit / (grad_norm + 1e-06))
    qkv_updated, qkv_first_new, qkv_second_new = adam_step(qkv_master, summed[0] * factor, qkv_first, qkv_second)
    out_updated, out_first_new, out_second_new = adam_step(out_master, summed[1] * factor, out_first, out_second)
    up_updated, up_first_new, up_second_new = adam_step(up_master, summed[2] * factor, up_first, up_second)
    down_updated, down_first_new, down_second_new = adam_step(down_master, summed[3] * factor, down_first, down_second)
    ada_updated, ada_first_new, ada_second_new = adam_step(ada_master, summed[4] * factor, ada_first, ada_second)
    return (activations, input_grad, grad_norm, qkv_updated, qkv_first_new, qkv_second_new, out_updated, out_first_new, out_second_new, up_updated, up_first_new, up_second_new, down_updated, down_first_new, down_second_new, ada_updated, ada_first_new, ada_second_new)
```

```python
import math

import jax
import jax.numpy as jnp
from jax import lax
from jax.sharding import Mesh, PartitionSpec as P

D = 1024
HEADS = 16
HEAD_DIM = 64
FF = 4096
FRAMES = 12
STEP = 10
BANDS = 4
OWN_COLS = D // BANDS
LANES = 128

beta_first = 0.9
beta_second = 0.99
learn_rate = 0.03
weight_decay = 0.01
adam_epsilon = 1e-08
clip_limit = 1.0
norm_epsilon = 1e-06
masked_score = -1000000000.0


def contract_rows(left, right, precision=None):
    return lax.dot_general(
        left,
        right,
        (((0,), (0,)), ((), ())),
        precision=precision,
        preferred_element_type=jnp.float32,
    )


def contract_cols(left, right):
    return lax.dot_general(
        left, right, (((1,), (1,)), ((), ())), preferred_element_type=jnp.float32
    )


def normalize(values):
    average = jnp.mean(values, axis=-1, keepdims=True)
    centred = values - average
    variance = jnp.mean(centred * centred, axis=-1, keepdims=True)
    return centred * lax.rsqrt(variance + norm_epsilon)


def modulate(residual, shift, scale):
    return normalize(residual) * (1.0 + scale[:, None, :]) + shift[:, None, :]


def to_half(tensor):
    return lax.ppermute(tensor, "half", [(0, 1), (1, 0)])


def to_pair(tensor):
    return lax.ppermute(tensor, "pair", [(0, 1), (1, 0)])


def to_both(tensor):
    return lax.ppermute(tensor, ("pair", "half"), [(0, 3), (1, 2), (2, 1), (3, 0)])


def band_sum(tensor):
    tensor = tensor + to_half(tensor)
    return tensor + to_pair(tensor)


def relative_order(blocks, pair, half):
    rest = blocks.shape[1:]
    blocks = blocks.reshape((2, 2) + rest)
    blocks = jnp.where(half == 1, blocks[:, ::-1], blocks)
    blocks = jnp.where(pair == 1, blocks[::-1], blocks)
    return blocks.reshape((BANDS,) + rest)


def heads_of(blocks):
    count, rows, _ = blocks.shape
    return blocks.reshape(count, rows, 2, HEAD_DIM).transpose(0, 2, 1, 3).reshape(-1, rows, HEAD_DIM)


def blocks_of(heads):
    count, rows, _ = heads.shape
    return heads.reshape(-1, 2, rows, HEAD_DIM).transpose(0, 2, 1, 3).reshape(-1, rows, LANES)


def valid_keys(count, rows, local_rows):
    return jnp.arange(rows, dtype=jnp.int32) % local_rows // (local_rows // FRAMES) < count[0]


def attend(count, projected, local_rows):
    rows = projected.shape[1]
    key_valid = valid_keys(count, rows, local_rows)
    heads = heads_of(projected).reshape(3, BANDS, rows, HEAD_DIM)

    def one_head(pieces):
        query, key, value = pieces

        def one_block(query_part):
            scores = jnp.where(
                key_valid[None, :], contract_cols(query_part, key) * 0.125, masked_score
            )
            maxima = jnp.max(scores, axis=1, keepdims=True)
            exponent = jnp.exp(scores - maxima)
            totals = jnp.sum(exponent, axis=1, keepdims=True)
            outcome = jnp.dot(
                exponent.astype(jnp.bfloat16), value, preferred_element_type=jnp.float32
            )
            return outcome / totals, (maxima + jnp.log(totals))[:, 0]

        outcome, logs = lax.map(one_block, query.reshape(BANDS, local_rows, HEAD_DIM))
        return outcome.reshape(rows, HEAD_DIM), logs

    outcome, logs = lax.map(one_head, (heads[0], heads[1], heads[2]))
    return blocks_of(outcome.astype(jnp.bfloat16)), (outcome, logs)


def attend_back(count, projected, grad_attended, raw, local_rows):
    rows = projected.shape[1]
    key_valid = valid_keys(count, rows, local_rows)
    heads = heads_of(projected).reshape(3, BANDS, rows, HEAD_DIM)
    outcome, logs = raw
    grads = heads_of(grad_attended)
    deltas = jnp.sum(outcome * grads.astype(jnp.float32), axis=-1).reshape(logs.shape)

    def one_head(pieces):
        query, key, value, log_head, delta_head, grad = pieces

        def one_block(running, inputs):
            key_sum, value_sum = running
            query_part, log_part, delta_part, grad_part = inputs
            scores = jnp.where(
                key_valid[None, :], contract_cols(query_part, key) * 0.125, masked_score
            )
            probability = jnp.exp(scores - log_part[:, None])
            grad_prob = contract_cols(grad_part, value)
            grad_scores = (probability * (grad_prob - delta_part[:, None])).astype(jnp.bfloat16)
            grad_query = jnp.dot(grad_scores, key, preferred_element_type=jnp.float32) * 0.125
            key_sum = key_sum + contract_rows(grad_scores, query_part) * 0.125
            value_sum = value_sum + contract_rows(probability.astype(jnp.bfloat16), grad_part)
            return (key_sum, value_sum), grad_query.astype(jnp.bfloat16)

        zero = jnp.zeros((rows, HEAD_DIM), jnp.float32)
        split = (BANDS, local_rows, HEAD_DIM)
        (key_sum, value_sum), grad_query = lax.scan(
            one_block, (zero, zero), (query.reshape(split), log_head, delta_head, grad.reshape(split))
        )
        return (
            grad_query.reshape(rows, HEAD_DIM),
            key_sum.astype(jnp.bfloat16),
            value_sum.astype(jnp.bfloat16),
        )

    results = lax.map(one_head, (*heads, logs, deltas, grads))
    return tuple(blocks_of(result) for result in results)


def to_columns(blocks):
    return blocks.transpose(1, 0, 2).reshape(blocks.shape[1], -1)


def to_blocks(tensor):
    return tensor.reshape(tensor.shape[0], -1, LANES).transpose(1, 0, 2)


def adam_step(master, clipped, first, second):
    first_new = beta_first * first + (1.0 - beta_first) * clipped
    second_new = beta_second * second + (1.0 - beta_second) * clipped * clipped
    first_hat = first_new / (1.0 - beta_first**STEP)
    second_hat = second_new / (1.0 - beta_second**STEP)
    updated = master - learn_rate * (
        first_hat / (jnp.sqrt(second_hat) + adam_epsilon) + weight_decay * master
    )
    return (updated, first_new, second_new)


def per_device(
    tokens,
    cotangent,
    frame_counts,
    noise_levels,
    qkv_master,
    out_master,
    up_master,
    down_master,
    ada_master,
    qkv_first,
    out_first,
    up_first,
    down_first,
    ada_first,
    qkv_second,
    out_second,
    up_second,
    down_second,
    ada_second,
):
    clips = lax.axis_size("clip")
    clip, pair, half = lax.axis_index("clip"), lax.axis_index("pair"), lax.axis_index("half")
    everywhere = ("clip", "pair", "half")
    masters = (qkv_master, out_master, up_master, down_master, ada_master)
    firsts = (qkv_first, out_first, up_first, down_first, ada_first)
    seconds = (qkv_second, out_second, up_second, down_second, ada_second)
    local_rows = tokens.shape[1]
    frame_rows = local_rows // FRAMES
    own_rows = qkv_master.shape[0]
    up_groups = FF // (2 * LANES)

    own_tokens = tokens[0]
    half_tokens = to_half(own_tokens)
    pair_tokens = to_pair(own_tokens)
    clip_tokens = jnp.stack([own_tokens, half_tokens, pair_tokens, to_half(pair_tokens)])

    condition = embed_levels(noise_levels[0]).astype(jnp.bfloat16)
    conditions = lax.all_gather(condition.reshape(-1, LANES), "clip", tiled=True)
    device = (clip * 2 + pair) * 2 + half
    condition = lax.dynamic_slice_in_dim(
        conditions.reshape(clips * FRAMES, D), device * own_rows, own_rows, axis=1
    )
    part = jnp.dot(condition, ada_master.astype(jnp.bfloat16), preferred_element_type=jnp.float32)
    part = part.reshape(clips, FRAMES, 6, D).transpose(0, 2, 1, 3)
    modulation = lax.psum_scatter(
        part.reshape(clips * 6 * FRAMES, D), "clip", scatter_dimension=0, tiled=True
    )
    modulation = band_sum(modulation)
    shift_one, scale_one, gate_one, shift_two, scale_two, gate_two = modulation.reshape(
        6, FRAMES, D
    )

    w_qkv = qkv_master.astype(jnp.bfloat16).reshape(own_rows, 3, BANDS, OWN_COLS)
    w_qkv = lax.all_to_all(w_qkv.transpose(2, 0, 1, 3), ("pair", "half"), 0, 0)
    w_qkv = lax.all_gather(w_qkv.reshape(BANDS * own_rows, 3 * OWN_COLS), "clip", tiled=True)

    up_low = up_master.astype(jnp.bfloat16).reshape(own_rows, up_groups, 2, LANES)
    mine = jnp.where(half == 0, up_low[:, :, 0], up_low[:, :, 1])
    other = to_half(jnp.where(half == 0, up_low[:, :, 1], up_low[:, :, 0]))
    up_low = jnp.where(half == 0, jnp.stack([mine, other]), jnp.stack([other, mine]))
    up_low = up_low.reshape(2 * own_rows, FF // 2)
    w_up = lax.all_gather(up_low, ("clip", "pair"), tiled=True)
    w_down = lax.all_gather(down_master.astype(jnp.bfloat16), ("clip", "pair"), tiled=True)
    w_out = lax.all_gather(out_master.astype(jnp.bfloat16), everywhere, tiled=True)
    w_out = relative_order(w_out.reshape(BANDS, OWN_COLS, D), pair, half).reshape(D, D)

    wide = clip_tokens.astype(jnp.float32).reshape(BANDS, FRAMES, frame_rows, D)
    normed = normalize(wide)
    first_in = normed * (1.0 + scale_one[None, :, None, :]) + shift_one[None, :, None, :]
    first_in = first_in.astype(jnp.bfloat16).reshape(BANDS * local_rows, D)
    projected = jnp.dot(first_in, w_qkv, preferred_element_type=jnp.float32).astype(jnp.bfloat16)
    projected = to_blocks(projected)
    attended, raw = attend(frame_counts, projected, local_rows)
    attended = attended.reshape(-1, BANDS, local_rows, LANES)
    attended = [attended[:, place] for place in range(BANDS)]
    attended = to_columns(
        jnp.concatenate(
            [attended[0], to_half(attended[1]), to_pair(attended[2]), to_both(attended[3])]
        )
    )

    residual = own_tokens.astype(jnp.float32).reshape(FRAMES, frame_rows, D)
    branch_one = jnp.dot(attended, w_out, preferred_element_type=jnp.float32).reshape(
        FRAMES, frame_rows, D
    )
    middle = residual + gate_one[:, None, :] * branch_one
    second_in = modulate(middle, shift_two, scale_two).astype(jnp.bfloat16).reshape(local_rows, D)
    upstream = cotangent[0].astype(jnp.float32).reshape(FRAMES, frame_rows, D)
    grad_branch_two = (gate_two[:, None, :] * upstream).astype(jnp.bfloat16).reshape(local_rows, D)
    second_both = jnp.concatenate([second_in, to_half(second_in)])
    grad_branch_both = jnp.concatenate([grad_branch_two, to_half(grad_branch_two)])

    pre_act = jnp.dot(second_both, w_up, preferred_element_type=jnp.float32)
    hidden, gelu_pullback = jax.vjp(lambda inner: jax.nn.gelu(inner, approximate=True), pre_act)
    hidden = hidden.astype(jnp.bfloat16)
    grad_hidden = contract_cols(grad_branch_both, w_down)
    grad_pre = gelu_pullback(grad_hidden)[0].astype(jnp.bfloat16)
    grad_second = contract_cols(grad_pre, w_up)
    grad_second = grad_second[:local_rows] + to_half(
        grad_second[local_rows:].astype(jnp.bfloat16)
    ).astype(jnp.float32)
    grad_second = grad_second.reshape(FRAMES, frame_rows, D)
    _, second_pullback = jax.vjp(modulate, middle, shift_two, scale_two)
    middle_part, grad_shift_two, grad_scale_two = second_pullback(grad_second)
    grad_middle = upstream + middle_part
    grad_branch_one = (
        (gate_one[:, None, :] * grad_middle).astype(jnp.bfloat16).reshape(local_rows, D)
    )
    grad_gate_one = jnp.sum(grad_middle * branch_one, axis=1)
    grad_attended = contract_cols(grad_branch_one, w_out).astype(jnp.bfloat16)
    pieces = to_blocks(grad_attended).reshape(BANDS, -1, local_rows, LANES)
    grad_attended = jnp.concatenate(
        [pieces[0], to_half(pieces[1]), to_pair(pieces[2]), to_both(pieces[3])], axis=1
    )

    branch_two = jnp.dot(hidden, w_down, preferred_element_type=jnp.float32)
    branch_two = branch_two[:local_rows] + to_half(
        branch_two[local_rows:].astype(jnp.bfloat16)
    ).astype(jnp.float32)
    branch_two = branch_two.reshape(FRAMES, frame_rows, D)
    activations = (
        (middle + gate_two[:, None, :] * branch_two).astype(jnp.bfloat16).reshape(1, local_rows, D)
    )
    grad_gate_two = jnp.sum(upstream * branch_two, axis=1)
    grad_down = contract_rows(hidden, grad_branch_both).astype(jnp.bfloat16)
    grad_down = lax.psum_scatter(grad_down, ("clip", "pair"), scatter_dimension=0, tiled=True)
    grad_up = contract_rows(second_both, grad_pre).astype(jnp.bfloat16)
    grad_up = lax.psum_scatter(grad_up, ("clip", "pair"), scatter_dimension=0, tiled=True)
    grad_out = contract_rows(attended, grad_branch_one).astype(jnp.bfloat16)
    grad_out = relative_order(grad_out.reshape(BANDS, OWN_COLS, D), pair, half).reshape(D, D)
    grad_out = lax.psum_scatter(grad_out, everywhere, scatter_dimension=0, tiled=True)
    early = jnp.concatenate([grad_gate_one, grad_shift_two, grad_scale_two, grad_gate_two])
    early = lax.all_gather(band_sum(early), "clip")

    grad_query, grad_key, grad_value = attend_back(
        frame_counts, projected, grad_attended, raw, local_rows
    )
    grad_projected = to_columns(jnp.concatenate([grad_query, grad_key, grad_value]))
    grad_qkv = contract_rows(first_in, grad_projected).astype(jnp.bfloat16)
    grad_qkv = lax.psum_scatter(grad_qkv, "clip", scatter_dimension=0, tiled=True)
    grad_first = contract_cols(grad_projected, w_qkv)
    grad_first = grad_first.reshape(BANDS, FRAMES, frame_rows, D)
    late = jnp.concatenate(
        [jnp.sum(grad_first, axis=(0, 2)), jnp.sum(grad_first * normed, axis=(0, 2))]
    )
    late = lax.all_gather(band_sum(late), "clip")
    low = grad_first.astype(jnp.bfloat16)
    own_part = grad_first[0] + to_half(low[1]).astype(jnp.float32)
    far_part = grad_first[2] + to_half(low[3]).astype(jnp.float32)
    grad_first = own_part + to_pair(far_part.astype(jnp.bfloat16)).astype(jnp.float32)
    _, first_pullback = jax.vjp(lambda inner: modulate(inner, shift_one, scale_one), residual)
    input_grad = (grad_middle + first_pullback(grad_first)[0]).reshape(1, local_rows, D)

    grad_qkv = grad_qkv.reshape(BANDS, own_rows, 3 * OWN_COLS)
    grad_qkv = lax.all_to_all(grad_qkv, ("pair", "half"), 0, 0)
    grad_qkv = grad_qkv.reshape(BANDS, own_rows, 3, OWN_COLS).transpose(1, 2, 0, 3)
    grad_qkv = grad_qkv.reshape(own_rows, 3 * D).astype(jnp.float32)
    grad_up = grad_up.reshape(2, own_rows, up_groups, LANES)
    mine = jnp.where(half == 0, grad_up[0], grad_up[1])
    other = to_half(jnp.where(half == 0, grad_up[1], grad_up[0]))
    grad_up = jnp.where(
        half == 0, jnp.stack([mine, other], axis=2), jnp.stack([other, mine], axis=2)
    )
    grad_up = grad_up.reshape(own_rows, FF).astype(jnp.float32)
    grad_modulation = jnp.concatenate([late, early], axis=1).reshape(clips, 6, FRAMES, D)
    grad_modulation = grad_modulation.transpose(0, 2, 1, 3).reshape(clips * FRAMES, 6 * D)
    grad_ada = contract_rows(
        condition.astype(jnp.float32), grad_modulation, precision=lax.Precision.HIGHEST
    )
    reduced = (
        grad_qkv,
        grad_out.astype(jnp.float32),
        grad_up,
        grad_down.astype(jnp.float32),
        grad_ada,
    )
    local_squares = sum((jnp.sum(piece * piece) for piece in reduced))
    grad_norm = jnp.sqrt(lax.psum(local_squares, everywhere))
    factor = jnp.minimum(1.0, clip_limit / (grad_norm + 1e-06))
    results = []
    for master, gradient, first, second in zip(masters, reduced, firsts, seconds):
        results.extend(adam_step(master, gradient * factor, first, second))
    return (activations, input_grad, grad_norm, *results)


def embed_levels(levels):
    halfway = D // 2
    spacing = jnp.exp(-math.log(10000.0) * jnp.arange(halfway, dtype=jnp.float32) / halfway)
    angles = levels.astype(jnp.float32)[..., None] * spacing
    return jax.nn.silu(jnp.concatenate([jnp.cos(angles), jnp.sin(angles)], axis=-1))


def solution(mesh):
    clips, bands = mesh.devices.shape
    split = Mesh(mesh.devices.reshape(clips, bands // 2, 2), ("clip", "pair", "half"))
    rows = P(("clip", "pair", "half"), None)
    activation = P("clip", ("pair", "half"), None)
    return jax.shard_map(
        per_device,
        mesh=split,
        in_specs=(activation, activation, P("clip"), P("clip", None)) + (rows,) * 15,
        out_specs=(activation, activation, P()) + (rows,) * 15,
        check_vma=False,
    )
```

```python
import math

import jax
import jax.numpy as jnp
from jax import lax
from jax.sharding import Mesh, PartitionSpec as P

D = 1024
HEADS = 16
HEAD_DIM = 64
FF = 4096
FRAMES = 12
STEP = 10
BANDS = 4
OWN_COLS = D // BANDS
LANES = 128

beta_first = 0.9
beta_second = 0.99
learn_rate = 0.03
weight_decay = 0.01
adam_epsilon = 1e-08
clip_limit = 1.0
norm_epsilon = 1e-06
masked_score = -1000000000.0


def contract_rows(left, right, precision=None):
    return lax.dot_general(
        left,
        right,
        (((0,), (0,)), ((), ())),
        precision=precision,
        preferred_element_type=jnp.float32,
    )


def contract_cols(left, right):
    return lax.dot_general(
        left, right, (((1,), (1,)), ((), ())), preferred_element_type=jnp.float32
    )


def normalize(values):
    average = jnp.mean(values, axis=-1, keepdims=True)
    centred = values - average
    variance = jnp.mean(centred * centred, axis=-1, keepdims=True)
    return centred * lax.rsqrt(variance + norm_epsilon)


def modulate(residual, shift, scale):
    return normalize(residual) * (1.0 + scale[:, None, :]) + shift[:, None, :]


def to_half(tensor):
    return lax.ppermute(tensor, "half", [(0, 1), (1, 0)])


def to_pair(tensor):
    return lax.ppermute(tensor, "pair", [(0, 1), (1, 0)])


def to_both(tensor):
    return lax.ppermute(tensor, ("pair", "half"), [(0, 3), (1, 2), (2, 1), (3, 0)])


def band_sum(tensor):
    tensor = tensor + to_half(tensor)
    return tensor + to_pair(tensor)


def clip_exchange(tensor, distance, clips):
    return lax.ppermute(tensor, "clip", [(place, place ^ distance) for place in range(clips)])


def clip_gather(tensor, clip, clips):
    distance = 1
    while distance < clips:
        other = clip_exchange(tensor, distance, clips)
        later = (clip // distance) % 2 == 1
        tensor = jnp.where(
            later, jnp.concatenate([other, tensor]), jnp.concatenate([tensor, other])
        )
        distance *= 2
    return tensor


def sum_everywhere(tensor, clips):
    tensor = band_sum(tensor)
    distance = 1
    while distance < clips:
        tensor = tensor + clip_exchange(tensor, distance, clips)
        distance *= 2
    return tensor


def in_order(own, other, index, axis=0):
    return jnp.where(
        index == 0, jnp.stack([own, other], axis=axis), jnp.stack([other, own], axis=axis)
    )


def relative_order(blocks, pair, half):
    rest = blocks.shape[1:]
    blocks = blocks.reshape((2, 2) + rest)
    blocks = jnp.where(half == 1, blocks[:, ::-1], blocks)
    blocks = jnp.where(pair == 1, blocks[::-1], blocks)
    return blocks.reshape((BANDS,) + rest)


def heads_of(tensor):
    return tensor.reshape(tensor.shape[0], -1, HEAD_DIM).transpose(1, 0, 2)


def columns_of(heads):
    return heads.transpose(1, 0, 2).reshape(heads.shape[1], -1)


def valid_keys(count, rows, local_rows):
    return jnp.arange(rows, dtype=jnp.int32) % local_rows // (local_rows // FRAMES) < count[0]


def attend(count, projected, local_rows):
    rows = projected.shape[0]
    key_valid = valid_keys(count, rows, local_rows)
    heads = heads_of(projected).reshape(3, BANDS, rows, HEAD_DIM)

    def one_head(pieces):
        query, key, value = pieces

        def one_block(query_part):
            scores = jnp.where(
                key_valid[None, :], contract_cols(query_part, key) * 0.125, masked_score
            )
            maxima = jnp.max(scores, axis=1, keepdims=True)
            exponent = jnp.exp(scores - maxima)
            totals = jnp.sum(exponent, axis=1, keepdims=True)
            outcome = jnp.dot(
                exponent.astype(jnp.bfloat16), value, preferred_element_type=jnp.float32
            )
            return outcome / totals, (maxima + jnp.log(totals))[:, 0]

        outcome, logs = lax.map(one_block, query.reshape(BANDS, local_rows, HEAD_DIM))
        return outcome.reshape(rows, HEAD_DIM), logs

    outcome, logs = lax.map(one_head, (heads[0], heads[1], heads[2]))
    return columns_of(outcome.astype(jnp.bfloat16)), (outcome, logs)


def attend_back(count, projected, grad_attended, raw, local_rows):
    rows = projected.shape[0]
    key_valid = valid_keys(count, rows, local_rows)
    heads = heads_of(projected).reshape(3, BANDS, rows, HEAD_DIM)
    outcome, logs = raw
    grads = heads_of(grad_attended)
    deltas = jnp.sum(outcome * grads.astype(jnp.float32), axis=-1).reshape(logs.shape)

    def one_head(pieces):
        query, key, value, log_head, delta_head, grad = pieces

        def one_block(running, inputs):
            key_sum, value_sum = running
            query_part, log_part, delta_part, grad_part = inputs
            scores = jnp.where(
                key_valid[None, :], contract_cols(query_part, key) * 0.125, masked_score
            )
            probability = jnp.exp(scores - log_part[:, None])
            grad_prob = contract_cols(grad_part, value)
            grad_scores = (probability * (grad_prob - delta_part[:, None])).astype(jnp.bfloat16)
            grad_query = jnp.dot(grad_scores, key, preferred_element_type=jnp.float32) * 0.125
            key_sum = key_sum + contract_rows(grad_scores, query_part) * 0.125
            value_sum = value_sum + contract_rows(probability.astype(jnp.bfloat16), grad_part)
            return (key_sum, value_sum), grad_query.astype(jnp.bfloat16)

        zero = jnp.zeros((rows, HEAD_DIM), jnp.float32)
        split = (BANDS, local_rows, HEAD_DIM)
        (key_sum, value_sum), grad_query = lax.scan(
            one_block, (zero, zero), (query.reshape(split), log_head, delta_head, grad.reshape(split))
        )
        return (
            grad_query.reshape(rows, HEAD_DIM),
            key_sum.astype(jnp.bfloat16),
            value_sum.astype(jnp.bfloat16),
        )

    results = lax.map(one_head, (*heads, logs, deltas, grads))
    return jnp.concatenate([columns_of(result) for result in results], axis=1)


def adam_step(master, clipped, first, second):
    first_new = beta_first * first + (1.0 - beta_first) * clipped
    second_new = beta_second * second + (1.0 - beta_second) * clipped * clipped
    first_hat = first_new / (1.0 - beta_first**STEP)
    second_hat = second_new / (1.0 - beta_second**STEP)
    updated = master - learn_rate * (
        first_hat / (jnp.sqrt(second_hat) + adam_epsilon) + weight_decay * master
    )
    return (updated, first_new, second_new)


def per_device(
    tokens,
    cotangent,
    frame_counts,
    noise_levels,
    qkv_master,
    out_master,
    up_master,
    down_master,
    ada_master,
    qkv_first,
    out_first,
    up_first,
    down_first,
    ada_first,
    qkv_second,
    out_second,
    up_second,
    down_second,
    ada_second,
):
    clips = lax.axis_size("clip")
    clip, pair, half = lax.axis_index("clip"), lax.axis_index("pair"), lax.axis_index("half")
    everywhere = ("clip", "pair", "half")
    masters = (qkv_master, out_master, up_master, down_master, ada_master)
    firsts = (qkv_first, out_first, up_first, down_first, ada_first)
    seconds = (qkv_second, out_second, up_second, down_second, ada_second)
    local_rows = tokens.shape[1]
    frame_rows = local_rows // FRAMES
    own_rows = qkv_master.shape[0]
    up_groups = FF // (2 * LANES)

    own_tokens = tokens[0]
    half_tokens = to_half(own_tokens)
    pair_tokens = to_pair(own_tokens)
    clip_tokens = jnp.stack([own_tokens, half_tokens, pair_tokens, to_half(pair_tokens)])

    w_first = jnp.concatenate(
        [
            qkv_master.astype(jnp.bfloat16)
            .reshape(own_rows, 3, BANDS, OWN_COLS)
            .transpose(2, 0, 1, 3)
            .reshape(BANDS, own_rows, 3 * OWN_COLS),
            ada_master.astype(jnp.bfloat16)
            .reshape(own_rows, BANDS, 6 * OWN_COLS)
            .transpose(1, 0, 2),
        ],
        axis=2,
    )
    w_first = lax.all_to_all(w_first, ("pair", "half"), 0, 0)
    w_first = lax.all_gather(w_first.reshape(BANDS * own_rows, 9 * OWN_COLS), "clip", tiled=True)
    w_qkv = w_first[:, : 3 * OWN_COLS]

    condition = embed_levels(noise_levels[0]).astype(jnp.bfloat16)
    modulation = jnp.dot(condition, w_first[:, 3 * OWN_COLS :], preferred_element_type=jnp.float32)
    modulation = in_order(modulation, to_half(modulation), half)
    modulation = in_order(modulation, to_pair(modulation), pair)
    modulation = modulation.reshape(BANDS, FRAMES, 6 * OWN_COLS).transpose(1, 0, 2)
    shift_one, scale_one, gate_one, shift_two, scale_two, gate_two = jnp.split(
        modulation.reshape(FRAMES, 6 * D), 6, axis=1
    )

    up_low = up_master.astype(jnp.bfloat16).reshape(own_rows, up_groups, 2, LANES)
    mine = jnp.where(half == 0, up_low[:, :, 0], up_low[:, :, 1])
    other = to_half(jnp.where(half == 0, up_low[:, :, 1], up_low[:, :, 0]))
    up_low = jnp.where(half == 0, jnp.stack([mine, other]), jnp.stack([other, mine]))
    up_low = up_low.reshape(2 * own_rows, FF // 2)
    w_up = lax.all_gather(up_low, ("clip", "pair"), tiled=True)
    w_down = lax.all_gather(down_master.astype(jnp.bfloat16), ("clip", "pair"), tiled=True)
    w_out = lax.all_gather(out_master.astype(jnp.bfloat16), everywhere, tiled=True)
    w_out = relative_order(w_out.reshape(BANDS, OWN_COLS, D), pair, half).reshape(D, D)

    wide = clip_tokens.astype(jnp.float32).reshape(BANDS, FRAMES, frame_rows, D)
    normed = normalize(wide)
    first_in = normed * (1.0 + scale_one[None, :, None, :]) + shift_one[None, :, None, :]
    first_in = first_in.astype(jnp.bfloat16).reshape(BANDS * local_rows, D)
    projected = jnp.dot(first_in, w_qkv, preferred_element_type=jnp.float32).astype(jnp.bfloat16)
    attended, raw = attend(frame_counts, projected, local_rows)
    attended = attended.reshape(BANDS, local_rows, OWN_COLS)
    attended = jnp.concatenate(
        [attended[0], to_half(attended[1]), to_pair(attended[2]), to_both(attended[3])], axis=1
    )

    residual = own_tokens.astype(jnp.float32).reshape(FRAMES, frame_rows, D)
    branch_one = jnp.dot(attended, w_out, preferred_element_type=jnp.float32).reshape(
        FRAMES, frame_rows, D
    )
    middle = residual + gate_one[:, None, :] * branch_one
    second_in = modulate(middle, shift_two, scale_two).astype(jnp.bfloat16).reshape(local_rows, D)
    upstream = cotangent[0].astype(jnp.float32).reshape(FRAMES, frame_rows, D)
    grad_branch_two = (gate_two[:, None, :] * upstream).astype(jnp.bfloat16).reshape(local_rows, D)
    second_both = jnp.concatenate([second_in, to_half(second_in)])
    grad_branch_both = jnp.concatenate([grad_branch_two, to_half(grad_branch_two)])

    pre_act = jnp.dot(second_both, w_up, preferred_element_type=jnp.float32)
    hidden, gelu_pullback = jax.vjp(lambda inner: jax.nn.gelu(inner, approximate=True), pre_act)
    hidden = hidden.astype(jnp.bfloat16)
    grad_hidden = contract_cols(grad_branch_both, w_down)
    grad_pre = gelu_pullback(grad_hidden)[0].astype(jnp.bfloat16)
    grad_second = contract_cols(grad_pre, w_up)
    grad_second = grad_second[:local_rows] + to_half(
        grad_second[local_rows:].astype(jnp.bfloat16)
    ).astype(jnp.float32)
    grad_second = grad_second.reshape(FRAMES, frame_rows, D)
    _, second_pullback = jax.vjp(modulate, middle, shift_two, scale_two)
    middle_part, grad_shift_two, grad_scale_two = second_pullback(grad_second)
    grad_middle = upstream + middle_part
    grad_branch_one = (
        (gate_one[:, None, :] * grad_middle).astype(jnp.bfloat16).reshape(local_rows, D)
    )
    grad_gate_one = jnp.sum(grad_middle * branch_one, axis=1)
    grad_attended = contract_cols(grad_branch_one, w_out).astype(jnp.bfloat16)
    pieces = jnp.split(grad_attended, BANDS, axis=1)
    grad_attended = jnp.concatenate(
        [pieces[0], to_half(pieces[1]), to_pair(pieces[2]), to_both(pieces[3])]
    )

    branch_two = jnp.dot(hidden, w_down, preferred_element_type=jnp.float32)
    branch_two = branch_two[:local_rows] + to_half(
        branch_two[local_rows:].astype(jnp.bfloat16)
    ).astype(jnp.float32)
    branch_two = branch_two.reshape(FRAMES, frame_rows, D)
    activations = (
        (middle + gate_two[:, None, :] * branch_two).astype(jnp.bfloat16).reshape(1, local_rows, D)
    )
    grad_gate_two = jnp.sum(upstream * branch_two, axis=1)
    groups = clips * (BANDS // 2)
    down_rows = down_master.shape[0]
    grad_down = contract_rows(hidden, grad_branch_both).astype(jnp.bfloat16)
    grad_up = contract_rows(second_both, grad_pre).astype(jnp.bfloat16)
    grad_out = contract_rows(attended, grad_branch_one)
    grad_out = relative_order(grad_out.reshape(BANDS, OWN_COLS, D), pair, half)
    grad_out = grad_out.reshape(groups, 2, own_rows, D)
    mine = jnp.where(half == 0, grad_out[:, 0], grad_out[:, 1])
    other = jnp.where(half == 0, grad_out[:, 1], grad_out[:, 0]).astype(jnp.bfloat16)
    grad_out = (mine + to_half(other).astype(jnp.float32)).astype(jnp.bfloat16)
    packed = jnp.concatenate(
        [
            grad_down.reshape(groups, down_rows, D),
            grad_up.reshape(groups, 2, own_rows, 2, D)
            .transpose(0, 1, 3, 2, 4)
            .reshape(groups, 4 * own_rows, D),
            grad_out,
        ],
        axis=1,
    )
    packed = lax.psum_scatter(
        packed.reshape(-1, D), ("clip", "pair"), scatter_dimension=0, tiled=True
    )
    early = band_sum(
        jnp.concatenate([grad_gate_one, grad_shift_two, grad_scale_two, grad_gate_two])
    )
    early = jnp.concatenate(
        [early, condition.astype(jnp.float32), jnp.zeros((4, D), jnp.float32)]
    )
    early = lax.all_gather(early, "clip")

    grad_projected = attend_back(frame_counts, projected, grad_attended, raw, local_rows)
    grad_projected, packed, early = lax.optimization_barrier((grad_projected, packed, early))
    grad_qkv = contract_rows(first_in, grad_projected).astype(jnp.bfloat16)
    grad_qkv = lax.psum_scatter(grad_qkv, "clip", scatter_dimension=0, tiled=True)
    grad_first = contract_cols(grad_projected, w_qkv)
    grad_first = grad_first.reshape(BANDS, FRAMES, frame_rows, D)
    late = jnp.concatenate(
        [jnp.sum(grad_first, axis=(0, 2)), jnp.sum(grad_first * normed, axis=(0, 2))]
    )
    late = clip_gather(band_sum(late), clip, clips).reshape(clips, 2 * FRAMES, D)
    low = grad_first.astype(jnp.bfloat16)
    own_part = grad_first[0] + to_half(low[1]).astype(jnp.float32)
    far_part = grad_first[2] + to_half(low[3]).astype(jnp.float32)
    grad_first = own_part + to_pair(far_part.astype(jnp.bfloat16)).astype(jnp.float32)
    _, first_pullback = jax.vjp(lambda inner: modulate(inner, shift_one, scale_one), residual)
    input_grad = (grad_middle + first_pullback(grad_first)[0]).reshape(1, local_rows, D)

    grad_qkv = grad_qkv.reshape(BANDS, own_rows, 3 * OWN_COLS)
    grad_qkv = lax.all_to_all(grad_qkv, ("pair", "half"), 0, 0)
    grad_qkv = grad_qkv.reshape(BANDS, own_rows, 3, OWN_COLS).transpose(1, 2, 0, 3)
    grad_qkv = grad_qkv.reshape(own_rows, 3 * D).astype(jnp.float32)
    grad_down = packed[:down_rows]
    grad_up = packed[down_rows : down_rows + 4 * own_rows].reshape(2, 2, own_rows, D)
    grad_out = packed[down_rows + 4 * own_rows :]
    mine = jnp.where(half == 0, grad_up[0], grad_up[1])
    other = to_half(jnp.where(half == 0, grad_up[1], grad_up[0]))

    def to_groups(tensor):
        tensor = tensor.transpose(1, 0, 2).reshape(own_rows, up_groups, LANES)
        return tensor

    grad_up = in_order(to_groups(mine), to_groups(other), half, axis=2)
    grad_up = grad_up.reshape(own_rows, FF).astype(jnp.float32)
    conditions = early[:, 4 * FRAMES : 5 * FRAMES].reshape(clips * FRAMES, D)
    grad_modulation = jnp.concatenate([late, early[:, : 4 * FRAMES]], axis=1)
    grad_modulation = grad_modulation.reshape(clips, 6, FRAMES, D)
    grad_modulation = grad_modulation.transpose(0, 2, 1, 3).reshape(clips * FRAMES, 6 * D)
    device = (clip * 2 + pair) * 2 + half
    grad_ada = contract_rows(
        lax.dynamic_slice_in_dim(conditions, device * own_rows, own_rows, axis=1),
        grad_modulation,
        precision=lax.Precision.HIGHEST,
    )
    reduced = (
        grad_qkv,
        grad_out.astype(jnp.float32),
        grad_up,
        grad_down.astype(jnp.float32),
        grad_ada,
    )
    local_squares = sum((jnp.sum(piece * piece) for piece in reduced))
    squares = sum_everywhere(jnp.full((8, LANES), local_squares), clips)
    grad_norm = jnp.sqrt(squares[0, 0])
    factor = jnp.minimum(1.0, clip_limit / (grad_norm + 1e-06))
    results = []
    for master, gradient, first, second in zip(masters, reduced, firsts, seconds):
        results.extend(adam_step(master, gradient * factor, first, second))
    return (activations, input_grad, grad_norm, *results)


def embed_levels(levels):
    halfway = D // 2
    spacing = jnp.exp(-math.log(10000.0) * jnp.arange(halfway, dtype=jnp.float32) / halfway)
    angles = levels.astype(jnp.float32)[..., None] * spacing
    return jax.nn.silu(jnp.concatenate([jnp.cos(angles), jnp.sin(angles)], axis=-1))


def solution(mesh):
    clips, bands = mesh.devices.shape
    split = Mesh(mesh.devices.reshape(clips, bands // 2, 2), ("clip", "pair", "half"))
    rows = P(("clip", "pair", "half"), None)
    activation = P("clip", ("pair", "half"), None)
    return jax.shard_map(
        per_device,
        mesh=split,
        in_specs=(activation, activation, P("clip"), P("clip", None)) + (rows,) * 15,
        out_specs=(activation, activation, P()) + (rows,) * 15,
        check_vma=False,
    )
```

```python
import math

import jax
import jax.numpy as jnp
from jax import lax
from jax.sharding import Mesh, PartitionSpec as P

D = 1024
HEADS = 16
HEAD_DIM = 64
FF = 4096
FRAMES = 12
STEP = 10
BANDS = 4
PARTS = 8
OWN_COLS = D // BANDS
LANES = 128

beta_first = 0.9
beta_second = 0.99
learn_rate = 0.03
weight_decay = 0.01
adam_epsilon = 1e-08
clip_limit = 1.0
norm_epsilon = 1e-06
masked_score = -1000000000.0


def contract_rows(left, right, precision=None):
    return lax.dot_general(
        left,
        right,
        (((0,), (0,)), ((), ())),
        precision=precision,
        preferred_element_type=jnp.float32,
    )


def contract_cols(left, right):
    return lax.dot_general(
        left, right, (((1,), (1,)), ((), ())), preferred_element_type=jnp.float32
    )


def normalize(values):
    average = jnp.mean(values, axis=-1, keepdims=True)
    centred = values - average
    variance = jnp.mean(centred * centred, axis=-1, keepdims=True)
    return centred * lax.rsqrt(variance + norm_epsilon)


def modulate(residual, shift, scale):
    return normalize(residual) * (1.0 + scale[:, None, :]) + shift[:, None, :]


def to_half(tensor):
    return lax.ppermute(tensor, "half", [(0, 1), (1, 0)])


def to_pair(tensor):
    return lax.ppermute(tensor, "pair", [(0, 1), (1, 0)])


def to_both(tensor):
    return lax.ppermute(tensor, ("pair", "half"), [(0, 3), (1, 2), (2, 1), (3, 0)])


def band_sum(tensor):
    tensor = tensor + to_half(tensor)
    return tensor + to_pair(tensor)


def clip_exchange(tensor, distance, clips):
    return lax.ppermute(tensor, "clip", [(place, place ^ distance) for place in range(clips)])


def clip_gather(tensor, clip, clips):
    distance = 1
    while distance < clips:
        other = clip_exchange(tensor, distance, clips)
        later = (clip // distance) % 2 == 1
        tensor = jnp.where(
            later, jnp.concatenate([other, tensor]), jnp.concatenate([tensor, other])
        )
        distance *= 2
    return tensor


def sum_everywhere(tensor, clips):
    tensor = band_sum(tensor)
    distance = 1
    while distance < clips:
        tensor = tensor + clip_exchange(tensor, distance, clips)
        distance *= 2
    return tensor


def in_order(own, other, index, axis=0):
    return jnp.where(
        index == 0, jnp.stack([own, other], axis=axis), jnp.stack([other, own], axis=axis)
    )


def relative_order(blocks, pair, half):
    rest = blocks.shape[1:]
    blocks = blocks.reshape((2, 2) + rest)
    blocks = jnp.where(half == 1, blocks[:, ::-1], blocks)
    blocks = jnp.where(pair == 1, blocks[::-1], blocks)
    return blocks.reshape((BANDS,) + rest)


def heads_of(tensor):
    return tensor.reshape(tensor.shape[0], -1, HEAD_DIM).transpose(1, 0, 2)


def columns_of(heads):
    return heads.transpose(1, 0, 2).reshape(heads.shape[1], -1)


def valid_keys(count, rows, local_rows):
    return jnp.arange(rows, dtype=jnp.int32) % local_rows // (local_rows // FRAMES) < count[0]


def attend(count, projected, local_rows):
    rows = projected.shape[0]
    key_valid = valid_keys(count, rows, local_rows)
    heads = heads_of(projected).reshape(3, BANDS, rows, HEAD_DIM)

    def one_head(pieces):
        query, key, value = pieces

        def one_block(query_part):
            scores = jnp.where(
                key_valid[None, :], contract_cols(query_part, key) * 0.125, masked_score
            )
            maxima = jnp.max(scores, axis=1, keepdims=True)
            exponent = jnp.exp(scores - maxima)
            totals = jnp.sum(exponent, axis=1, keepdims=True)
            outcome = jnp.dot(
                exponent.astype(jnp.bfloat16), value, preferred_element_type=jnp.float32
            )
            return outcome / totals, (maxima + jnp.log(totals))[:, 0]

        outcome, logs = lax.map(one_block, query.reshape(PARTS, rows // PARTS, HEAD_DIM))
        return outcome.reshape(rows, HEAD_DIM), logs

    outcome, logs = lax.map(one_head, (heads[0], heads[1], heads[2]))
    return columns_of(outcome.astype(jnp.bfloat16)), (outcome, logs)


def attend_back(count, projected, grad_attended, raw, local_rows):
    rows = projected.shape[0]
    key_valid = valid_keys(count, rows, local_rows)
    heads = heads_of(projected).reshape(3, BANDS, rows, HEAD_DIM)
    outcome, logs = raw
    grads = heads_of(grad_attended)
    deltas = jnp.sum(outcome * grads.astype(jnp.float32), axis=-1).reshape(logs.shape)

    def one_head(pieces):
        query, key, value, log_head, delta_head, grad = pieces

        def one_block(running, inputs):
            key_sum, value_sum = running
            query_part, log_part, delta_part, grad_part = inputs
            scores = jnp.where(
                key_valid[None, :], contract_cols(query_part, key) * 0.125, masked_score
            )
            probability = jnp.exp(scores - log_part[:, None])
            grad_prob = contract_cols(grad_part, value)
            grad_scores = (probability * (grad_prob - delta_part[:, None])).astype(jnp.bfloat16)
            grad_query = jnp.dot(grad_scores, key, preferred_element_type=jnp.float32) * 0.125
            key_sum = key_sum + contract_rows(grad_scores, query_part) * 0.125
            value_sum = value_sum + contract_rows(probability.astype(jnp.bfloat16), grad_part)
            return (key_sum, value_sum), grad_query.astype(jnp.bfloat16)

        zero = jnp.zeros((rows, HEAD_DIM), jnp.float32)
        split = (PARTS, rows // PARTS, HEAD_DIM)
        (key_sum, value_sum), grad_query = lax.scan(
            one_block, (zero, zero), (query.reshape(split), log_head, delta_head, grad.reshape(split))
        )
        return (
            grad_query.reshape(rows, HEAD_DIM),
            key_sum.astype(jnp.bfloat16),
            value_sum.astype(jnp.bfloat16),
        )

    results = lax.map(one_head, (*heads, logs, deltas, grads))
    return jnp.concatenate([columns_of(result) for result in results], axis=1)


def adam_step(master, clipped, first, second):
    first_new = beta_first * first + (1.0 - beta_first) * clipped
    second_new = beta_second * second + (1.0 - beta_second) * clipped * clipped
    first_hat = first_new / (1.0 - beta_first**STEP)
    second_hat = second_new / (1.0 - beta_second**STEP)
    updated = master - learn_rate * (
        first_hat / (jnp.sqrt(second_hat) + adam_epsilon) + weight_decay * master
    )
    return (updated, first_new, second_new)


def per_device(
    tokens,
    cotangent,
    frame_counts,
    noise_levels,
    qkv_master,
    out_master,
    up_master,
    down_master,
    ada_master,
    qkv_first,
    out_first,
    up_first,
    down_first,
    ada_first,
    qkv_second,
    out_second,
    up_second,
    down_second,
    ada_second,
):
    clips = lax.axis_size("clip")
    clip, pair, half = lax.axis_index("clip"), lax.axis_index("pair"), lax.axis_index("half")
    everywhere = ("clip", "pair", "half")
    masters = (qkv_master, out_master, up_master, down_master, ada_master)
    firsts = (qkv_first, out_first, up_first, down_first, ada_first)
    seconds = (qkv_second, out_second, up_second, down_second, ada_second)
    local_rows = tokens.shape[1]
    frame_rows = local_rows // FRAMES
    own_rows = qkv_master.shape[0]
    up_groups = FF // (2 * LANES)

    own_tokens = tokens[0]
    half_tokens = to_half(own_tokens)
    pair_tokens = to_pair(own_tokens)
    clip_tokens = jnp.stack([own_tokens, half_tokens, pair_tokens, to_half(pair_tokens)])

    w_first = jnp.concatenate(
        [
            qkv_master.astype(jnp.bfloat16)
            .reshape(own_rows, 3, BANDS, OWN_COLS)
            .transpose(2, 0, 1, 3)
            .reshape(BANDS, own_rows, 3 * OWN_COLS),
            ada_master.astype(jnp.bfloat16)
            .reshape(own_rows, BANDS, 6 * OWN_COLS)
            .transpose(1, 0, 2),
        ],
        axis=2,
    )
    w_first = lax.all_to_all(w_first, ("pair", "half"), 0, 0)
    w_first = lax.all_gather(w_first.reshape(BANDS * own_rows, 9 * OWN_COLS), "clip", tiled=True)
    w_qkv = w_first[:, : 3 * OWN_COLS]

    condition = embed_levels(noise_levels[0]).astype(jnp.bfloat16)
    modulation = jnp.dot(condition, w_first[:, 3 * OWN_COLS :], preferred_element_type=jnp.float32)
    modulation = in_order(modulation, to_half(modulation), half)
    modulation = in_order(modulation, to_pair(modulation), pair)
    modulation = modulation.reshape(BANDS, FRAMES, 6 * OWN_COLS).transpose(1, 0, 2)
    shift_one, scale_one, gate_one, shift_two, scale_two, gate_two = jnp.split(
        modulation.reshape(FRAMES, 6 * D), 6, axis=1
    )

    groups = clips * (BANDS // 2)
    down_rows = down_master.shape[0]
    up_low = up_master.astype(jnp.bfloat16).reshape(own_rows, up_groups, 2, LANES)
    mine = jnp.where(half == 0, up_low[:, :, 0], up_low[:, :, 1]).reshape(own_rows, FF // 2)
    other = jnp.where(half == 0, up_low[:, :, 1], up_low[:, :, 0]).reshape(own_rows, FF // 2)
    up_low = in_order(mine, to_half(other), half).reshape(2, own_rows, 2, D)
    up_low = up_low.transpose(0, 2, 1, 3).reshape(4 * own_rows, D)
    w_rest = jnp.concatenate(
        [down_master.astype(jnp.bfloat16), up_low, out_master.astype(jnp.bfloat16)]
    )
    w_rest = lax.all_gather(w_rest, ("clip", "pair"))
    w_out = w_rest[:, down_rows + 4 * own_rows :]
    w_out = in_order(w_out, to_half(w_out), half, axis=1)
    w_out = relative_order(w_out.reshape(BANDS, OWN_COLS, D), pair, half).reshape(D, D)
    w_down = w_rest[:, :down_rows].reshape(FF // 2, D)
    w_up = w_rest[:, down_rows : down_rows + 4 * own_rows].reshape(groups, 2, 2, own_rows, D)
    w_up = w_up.transpose(0, 1, 3, 2, 4).reshape(D, FF // 2)

    wide = clip_tokens.astype(jnp.float32).reshape(BANDS, FRAMES, frame_rows, D)
    normed = normalize(wide)
    first_in = normed * (1.0 + scale_one[None, :, None, :]) + shift_one[None, :, None, :]
    first_in = first_in.astype(jnp.bfloat16).reshape(BANDS * local_rows, D)
    projected = jnp.dot(first_in, w_qkv, preferred_element_type=jnp.float32).astype(jnp.bfloat16)
    attended, raw = attend(frame_counts, projected, local_rows)
    attended = attended.reshape(BANDS, local_rows, OWN_COLS)
    attended = jnp.concatenate(
        [attended[0], to_half(attended[1]), to_pair(attended[2]), to_both(attended[3])], axis=1
    )

    residual = own_tokens.astype(jnp.float32).reshape(FRAMES, frame_rows, D)
    branch_one = jnp.dot(attended, w_out, preferred_element_type=jnp.float32).reshape(
        FRAMES, frame_rows, D
    )
    middle = residual + gate_one[:, None, :] * branch_one
    second_in = modulate(middle, shift_two, scale_two).astype(jnp.bfloat16).reshape(local_rows, D)
    upstream = cotangent[0].astype(jnp.float32).reshape(FRAMES, frame_rows, D)
    grad_branch_two = (gate_two[:, None, :] * upstream).astype(jnp.bfloat16).reshape(local_rows, D)
    second_both = jnp.concatenate([second_in, to_half(second_in)])
    grad_branch_both = jnp.concatenate([grad_branch_two, to_half(grad_branch_two)])

    pre_act = jnp.dot(second_both, w_up, preferred_element_type=jnp.float32)
    hidden, gelu_pullback = jax.vjp(lambda inner: jax.nn.gelu(inner, approximate=True), pre_act)
    hidden = hidden.astype(jnp.bfloat16)
    grad_hidden = contract_cols(grad_branch_both, w_down)
    grad_pre = gelu_pullback(grad_hidden)[0].astype(jnp.bfloat16)
    grad_second = contract_cols(grad_pre, w_up)
    grad_second = grad_second[:local_rows] + to_half(
        grad_second[local_rows:].astype(jnp.bfloat16)
    ).astype(jnp.float32)
    grad_second = grad_second.reshape(FRAMES, frame_rows, D)
    _, second_pullback = jax.vjp(modulate, middle, shift_two, scale_two)
    middle_part, grad_shift_two, grad_scale_two = second_pullback(grad_second)
    grad_middle = upstream + middle_part
    grad_branch_one = (
        (gate_one[:, None, :] * grad_middle).astype(jnp.bfloat16).reshape(local_rows, D)
    )
    grad_gate_one = jnp.sum(grad_middle * branch_one, axis=1)
    grad_attended = contract_cols(grad_branch_one, w_out).astype(jnp.bfloat16)
    pieces = jnp.split(grad_attended, BANDS, axis=1)
    grad_attended = jnp.concatenate(
        [pieces[0], to_half(pieces[1]), to_pair(pieces[2]), to_both(pieces[3])]
    )

    branch_two = jnp.dot(hidden, w_down, preferred_element_type=jnp.float32)
    branch_two = branch_two[:local_rows] + to_half(
        branch_two[local_rows:].astype(jnp.bfloat16)
    ).astype(jnp.float32)
    branch_two = branch_two.reshape(FRAMES, frame_rows, D)
    activations = (
        (middle + gate_two[:, None, :] * branch_two).astype(jnp.bfloat16).reshape(1, local_rows, D)
    )
    grad_gate_two = jnp.sum(upstream * branch_two, axis=1)
    grad_down = contract_rows(hidden, grad_branch_both).astype(jnp.bfloat16)
    grad_up = contract_rows(second_both, grad_pre).astype(jnp.bfloat16)
    grad_out = contract_rows(attended, grad_branch_one)
    grad_out = relative_order(grad_out.reshape(BANDS, OWN_COLS, D), pair, half)
    grad_out = grad_out.reshape(groups, 2, own_rows, D)
    mine = jnp.where(half == 0, grad_out[:, 0], grad_out[:, 1])
    other = jnp.where(half == 0, grad_out[:, 1], grad_out[:, 0]).astype(jnp.bfloat16)
    grad_out = (mine + to_half(other).astype(jnp.float32)).astype(jnp.bfloat16)
    packed = jnp.concatenate(
        [
            grad_down.reshape(groups, down_rows, D),
            grad_up.reshape(groups, 2, own_rows, 2, D)
            .transpose(0, 1, 3, 2, 4)
            .reshape(groups, 4 * own_rows, D),
            grad_out,
        ],
        axis=1,
    )
    packed = lax.psum_scatter(
        packed.reshape(-1, D), ("clip", "pair"), scatter_dimension=0, tiled=True
    )
    early = band_sum(
        jnp.concatenate([grad_gate_one, grad_shift_two, grad_scale_two, grad_gate_two])
    )
    early = jnp.concatenate(
        [early, condition.astype(jnp.float32), jnp.zeros((4, D), jnp.float32)]
    )
    early = lax.all_gather(early, "clip")

    grad_projected = attend_back(frame_counts, projected, grad_attended, raw, local_rows)
    grad_projected, packed, early = lax.optimization_barrier((grad_projected, packed, early))
    grad_qkv = contract_rows(first_in, grad_projected).astype(jnp.bfloat16)
    grad_qkv = lax.psum_scatter(grad_qkv, "clip", scatter_dimension=0, tiled=True)
    grad_first = contract_cols(grad_projected, w_qkv)
    grad_first = grad_first.reshape(BANDS, FRAMES, frame_rows, D)
    late = jnp.concatenate(
        [jnp.sum(grad_first, axis=(0, 2)), jnp.sum(grad_first * normed, axis=(0, 2))]
    )
    late = clip_gather(band_sum(late), clip, clips).reshape(clips, 2 * FRAMES, D)
    low = grad_first.astype(jnp.bfloat16)
    own_part = grad_first[0] + to_half(low[1]).astype(jnp.float32)
    far_part = grad_first[2] + to_half(low[3]).astype(jnp.float32)
    grad_first = own_part + to_pair(far_part.astype(jnp.bfloat16)).astype(jnp.float32)
    _, first_pullback = jax.vjp(lambda inner: modulate(inner, shift_one, scale_one), residual)
    input_grad = (grad_middle + first_pullback(grad_first)[0]).reshape(1, local_rows, D)

    grad_qkv = grad_qkv.reshape(BANDS, own_rows, 3 * OWN_COLS)
    grad_qkv = lax.all_to_all(grad_qkv, ("pair", "half"), 0, 0)
    grad_qkv = grad_qkv.reshape(BANDS, own_rows, 3, OWN_COLS).transpose(1, 2, 0, 3)
    grad_qkv = grad_qkv.reshape(own_rows, 3 * D).astype(jnp.float32)
    grad_down = packed[:down_rows]
    grad_up = packed[down_rows : down_rows + 4 * own_rows].reshape(2, 2, own_rows, D)
    grad_out = packed[down_rows + 4 * own_rows :]
    mine = jnp.where(half == 0, grad_up[0], grad_up[1])
    other = to_half(jnp.where(half == 0, grad_up[1], grad_up[0]))

    def to_groups(tensor):
        tensor = tensor.transpose(1, 0, 2).reshape(own_rows, up_groups, LANES)
        return tensor

    grad_up = in_order(to_groups(mine), to_groups(other), half, axis=2)
    grad_up = grad_up.reshape(own_rows, FF).astype(jnp.float32)
    conditions = early[:, 4 * FRAMES : 5 * FRAMES].reshape(clips * FRAMES, D)
    grad_modulation = jnp.concatenate([late, early[:, : 4 * FRAMES]], axis=1)
    grad_modulation = grad_modulation.reshape(clips, 6, FRAMES, D)
    grad_modulation = grad_modulation.transpose(0, 2, 1, 3).reshape(clips * FRAMES, 6 * D)
    device = (clip * 2 + pair) * 2 + half
    grad_ada = contract_rows(
        lax.dynamic_slice_in_dim(conditions, device * own_rows, own_rows, axis=1),
        grad_modulation,
        precision=lax.Precision.HIGHEST,
    )
    reduced = (
        grad_qkv,
        grad_out.astype(jnp.float32),
        grad_up,
        grad_down.astype(jnp.float32),
        grad_ada,
    )
    local_squares = sum((jnp.sum(piece * piece) for piece in reduced))
    squares = sum_everywhere(jnp.full((8, LANES), local_squares), clips)
    grad_norm = jnp.sqrt(squares[0, 0])
    factor = jnp.minimum(1.0, clip_limit / (grad_norm + 1e-06))
    results = []
    for master, gradient, first, second in zip(masters, reduced, firsts, seconds):
        results.extend(adam_step(master, gradient * factor, first, second))
    return (activations, input_grad, grad_norm, *results)


def embed_levels(levels):
    halfway = D // 2
    spacing = jnp.exp(-math.log(10000.0) * jnp.arange(halfway, dtype=jnp.float32) / halfway)
    angles = levels.astype(jnp.float32)[..., None] * spacing
    return jax.nn.silu(jnp.concatenate([jnp.cos(angles), jnp.sin(angles)], axis=-1))


def solution(mesh):
    clips, bands = mesh.devices.shape
    split = Mesh(mesh.devices.reshape(clips, bands // 2, 2), ("clip", "pair", "half"))
    rows = P(("clip", "pair", "half"), None)
    activation = P("clip", ("pair", "half"), None)
    return jax.shard_map(
        per_device,
        mesh=split,
        in_specs=(activation, activation, P("clip"), P("clip", None)) + (rows,) * 15,
        out_specs=(activation, activation, P()) + (rows,) * 15,
        check_vma=False,
    )
```

```python
import math

import jax
import jax.numpy as jnp
from jax import lax
from jax.sharding import Mesh, PartitionSpec as P

D = 1024
HEADS = 16
HEAD_DIM = 64
FF = 4096
FRAMES = 12
STEP = 10
BANDS = 4
OWN_COLS = D // BANDS
LANES = 128

beta_first = 0.9
beta_second = 0.99
learn_rate = 0.03
weight_decay = 0.01
adam_epsilon = 1e-08
clip_limit = 1.0
norm_epsilon = 1e-06
masked_score = -1000000000.0


def contract_rows(left, right, precision=None):
    return lax.dot_general(
        left,
        right,
        (((0,), (0,)), ((), ())),
        precision=precision,
        preferred_element_type=jnp.float32,
    )


def contract_cols(left, right):
    return lax.dot_general(
        left, right, (((1,), (1,)), ((), ())), preferred_element_type=jnp.float32
    )


def normalize(values):
    average = jnp.mean(values, axis=-1, keepdims=True)
    centred = values - average
    variance = jnp.mean(centred * centred, axis=-1, keepdims=True)
    return centred * lax.rsqrt(variance + norm_epsilon)


def modulate(residual, shift, scale):
    return normalize(residual) * (1.0 + scale[:, None, :]) + shift[:, None, :]


def to_half(tensor):
    return lax.ppermute(tensor, "half", [(0, 1), (1, 0)])


def to_pair(tensor):
    return lax.ppermute(tensor, "pair", [(0, 1), (1, 0)])


def to_both(tensor):
    return lax.ppermute(tensor, ("pair", "half"), [(0, 3), (1, 2), (2, 1), (3, 0)])


def band_sum(tensor):
    tensor = tensor + to_half(tensor)
    return tensor + to_pair(tensor)


def clip_exchange(tensor, distance, clips):
    return lax.ppermute(tensor, "clip", [(place, place ^ distance) for place in range(clips)])


def clip_gather(tensor, clip, clips):
    distance = 1
    while distance < clips:
        other = clip_exchange(tensor, distance, clips)
        later = (clip // distance) % 2 == 1
        tensor = jnp.where(
            later, jnp.concatenate([other, tensor]), jnp.concatenate([tensor, other])
        )
        distance *= 2
    return tensor


def sum_everywhere(tensor, clips):
    tensor = band_sum(tensor)
    distance = 1
    while distance < clips:
        tensor = tensor + clip_exchange(tensor, distance, clips)
        distance *= 2
    return tensor


def in_order(own, other, index, axis=0):
    return jnp.where(
        index == 0, jnp.stack([own, other], axis=axis), jnp.stack([other, own], axis=axis)
    )


def relative_order(blocks, pair, half):
    rest = blocks.shape[1:]
    blocks = blocks.reshape((2, 2) + rest)
    blocks = jnp.where(half == 1, blocks[:, ::-1], blocks)
    blocks = jnp.where(pair == 1, blocks[::-1], blocks)
    return blocks.reshape((BANDS,) + rest)


def heads_of(tensor):
    return tensor.reshape(tensor.shape[0], -1, HEAD_DIM).transpose(1, 0, 2)


def columns_of(heads):
    return heads.transpose(1, 0, 2).reshape(heads.shape[1], -1)


def valid_keys(count, rows, local_rows):
    return jnp.arange(rows, dtype=jnp.int32) % local_rows // (local_rows // FRAMES) < count[0]


def attend(count, projected, local_rows):
    rows = projected.shape[0]
    key_valid = valid_keys(count, rows, local_rows)
    heads = heads_of(projected).reshape(3, BANDS, rows, HEAD_DIM)

    def one_head(pieces):
        query, key, value = pieces

        def one_block(query_part):
            scores = jnp.where(
                key_valid[None, :], contract_cols(query_part, key) * 0.125, masked_score
            )
            maxima = jnp.max(scores, axis=1, keepdims=True)
            exponent = jnp.exp(scores - maxima)
            totals = jnp.sum(exponent, axis=1, keepdims=True)
            outcome = jnp.dot(
                exponent.astype(jnp.bfloat16), value, preferred_element_type=jnp.float32
            )
            return outcome / totals, (maxima + jnp.log(totals))[:, 0]

        parts = []
        for part in jnp.split(query, BANDS):
            if parts:
                part, parts[-1] = lax.optimization_barrier((part, parts[-1]))
            parts.append(one_block(part))
        return jnp.concatenate([part[0] for part in parts]), jnp.stack([part[1] for part in parts])

    outcome, logs = lax.map(one_head, (heads[0], heads[1], heads[2]))
    return columns_of(outcome.astype(jnp.bfloat16)), (outcome, logs)


def attend_back(count, projected, grad_attended, raw, local_rows):
    rows = projected.shape[0]
    key_valid = valid_keys(count, rows, local_rows)
    heads = heads_of(projected).reshape(3, BANDS, rows, HEAD_DIM)
    outcome, logs = raw
    grads = heads_of(grad_attended)
    deltas = jnp.sum(outcome * grads.astype(jnp.float32), axis=-1).reshape(logs.shape)

    def one_head(pieces):
        query, key, value, log_head, delta_head, grad = pieces

        def one_block(running, inputs):
            key_sum, value_sum = running
            query_part, log_part, delta_part, grad_part = inputs
            scores = jnp.where(
                key_valid[None, :], contract_cols(query_part, key) * 0.125, masked_score
            )
            probability = jnp.exp(scores - log_part[:, None])
            grad_prob = contract_cols(grad_part, value)
            grad_scores = (probability * (grad_prob - delta_part[:, None])).astype(jnp.bfloat16)
            grad_query = jnp.dot(grad_scores, key, preferred_element_type=jnp.float32) * 0.125
            key_sum = key_sum + contract_rows(grad_scores, query_part) * 0.125
            value_sum = value_sum + contract_rows(probability.astype(jnp.bfloat16), grad_part)
            return (key_sum, value_sum), grad_query.astype(jnp.bfloat16)

        running = (0.0, 0.0)
        grad_query = []
        for place in range(BANDS):
            part = slice(place * local_rows, (place + 1) * local_rows)
            running, grad_part = one_block(
                running, (query[part], log_head[place], delta_head[place], grad[part])
            )
            grad_query.append(grad_part)
        key_sum, value_sum = running
        return (
            jnp.concatenate(grad_query),
            key_sum.astype(jnp.bfloat16),
            value_sum.astype(jnp.bfloat16),
        )

    results = lax.map(one_head, (*heads, logs, deltas, grads))
    return jnp.concatenate([columns_of(result) for result in results], axis=1)


def adam_step(master, clipped, first, second):
    first_new = beta_first * first + (1.0 - beta_first) * clipped
    second_new = beta_second * second + (1.0 - beta_second) * clipped * clipped
    first_hat = first_new / (1.0 - beta_first**STEP)
    second_hat = second_new / (1.0 - beta_second**STEP)
    updated = master - learn_rate * (
        first_hat / (jnp.sqrt(second_hat) + adam_epsilon) + weight_decay * master
    )
    return (updated, first_new, second_new)


def per_device(
    tokens,
    cotangent,
    frame_counts,
    noise_levels,
    qkv_master,
    out_master,
    up_master,
    down_master,
    ada_master,
    qkv_first,
    out_first,
    up_first,
    down_first,
    ada_first,
    qkv_second,
    out_second,
    up_second,
    down_second,
    ada_second,
):
    clips = lax.axis_size("clip")
    clip, pair, half = lax.axis_index("clip"), lax.axis_index("pair"), lax.axis_index("half")
    everywhere = ("clip", "pair", "half")
    masters = (qkv_master, out_master, up_master, down_master, ada_master)
    firsts = (qkv_first, out_first, up_first, down_first, ada_first)
    seconds = (qkv_second, out_second, up_second, down_second, ada_second)
    local_rows = tokens.shape[1]
    frame_rows = local_rows // FRAMES
    own_rows = qkv_master.shape[0]
    up_groups = FF // (2 * LANES)

    own_tokens = tokens[0]
    half_tokens = to_half(own_tokens)
    pair_tokens = to_pair(own_tokens)
    clip_tokens = jnp.stack([own_tokens, half_tokens, pair_tokens, to_half(pair_tokens)])

    w_first = jnp.concatenate(
        [
            qkv_master.astype(jnp.bfloat16)
            .reshape(own_rows, 3, BANDS, OWN_COLS)
            .transpose(2, 0, 1, 3)
            .reshape(BANDS, own_rows, 3 * OWN_COLS),
            ada_master.astype(jnp.bfloat16)
            .reshape(own_rows, BANDS, 6 * OWN_COLS)
            .transpose(1, 0, 2),
        ],
        axis=2,
    )
    w_first = lax.all_to_all(w_first, ("pair", "half"), 0, 0)
    w_first = lax.all_gather(w_first.reshape(BANDS * own_rows, 9 * OWN_COLS), "clip", tiled=True)
    w_qkv = w_first[:, : 3 * OWN_COLS]

    condition = embed_levels(noise_levels[0]).astype(jnp.bfloat16)
    modulation = jnp.dot(condition, w_first[:, 3 * OWN_COLS :], preferred_element_type=jnp.float32)
    modulation = in_order(modulation, to_half(modulation), half)
    modulation = in_order(modulation, to_pair(modulation), pair)
    modulation = modulation.reshape(BANDS, FRAMES, 6 * OWN_COLS).transpose(1, 0, 2)
    shift_one, scale_one, gate_one, shift_two, scale_two, gate_two = jnp.split(
        modulation.reshape(FRAMES, 6 * D), 6, axis=1
    )

    groups = clips * (BANDS // 2)
    down_rows = down_master.shape[0]
    up_low = up_master.astype(jnp.bfloat16).reshape(own_rows, up_groups, 2, LANES)
    mine = jnp.where(half == 0, up_low[:, :, 0], up_low[:, :, 1]).reshape(own_rows, FF // 2)
    other = jnp.where(half == 0, up_low[:, :, 1], up_low[:, :, 0]).reshape(own_rows, FF // 2)
    up_low = in_order(mine, to_half(other), half).reshape(2, own_rows, 2, D)
    up_low = up_low.transpose(0, 2, 1, 3).reshape(4 * own_rows, D)
    w_rest = jnp.concatenate(
        [down_master.astype(jnp.bfloat16), up_low, out_master.astype(jnp.bfloat16)]
    )
    w_rest = lax.all_gather(w_rest, ("clip", "pair"))
    w_out = w_rest[:, down_rows + 4 * own_rows :]
    w_out = in_order(w_out, to_half(w_out), half, axis=1)
    w_out = relative_order(w_out.reshape(BANDS, OWN_COLS, D), pair, half).reshape(D, D)
    w_down = w_rest[:, :down_rows].reshape(FF // 2, D)
    w_up = w_rest[:, down_rows : down_rows + 4 * own_rows].reshape(groups, 2, 2, own_rows, D)
    w_up = w_up.transpose(0, 1, 3, 2, 4).reshape(D, FF // 2)

    wide = clip_tokens.astype(jnp.float32).reshape(BANDS, FRAMES, frame_rows, D)
    normed = normalize(wide)
    first_in = normed * (1.0 + scale_one[None, :, None, :]) + shift_one[None, :, None, :]
    first_in = first_in.astype(jnp.bfloat16).reshape(BANDS * local_rows, D)
    projected = jnp.dot(first_in, w_qkv, preferred_element_type=jnp.float32).astype(jnp.bfloat16)
    attended, raw = attend(frame_counts, projected, local_rows)
    attended = attended.reshape(BANDS, local_rows, OWN_COLS)
    attended = jnp.concatenate(
        [attended[0], to_half(attended[1]), to_pair(attended[2]), to_both(attended[3])], axis=1
    )

    residual = own_tokens.astype(jnp.float32).reshape(FRAMES, frame_rows, D)
    branch_one = jnp.dot(attended, w_out, preferred_element_type=jnp.float32).reshape(
        FRAMES, frame_rows, D
    )
    middle = residual + gate_one[:, None, :] * branch_one
    second_in = modulate(middle, shift_two, scale_two).astype(jnp.bfloat16).reshape(local_rows, D)
    upstream = cotangent[0].astype(jnp.float32).reshape(FRAMES, frame_rows, D)
    grad_branch_two = (gate_two[:, None, :] * upstream).astype(jnp.bfloat16).reshape(local_rows, D)
    second_both = jnp.concatenate([second_in, to_half(second_in)])
    grad_branch_both = jnp.concatenate([grad_branch_two, to_half(grad_branch_two)])

    pre_act = jnp.dot(second_both, w_up, preferred_element_type=jnp.float32)
    hidden, gelu_pullback = jax.vjp(lambda inner: jax.nn.gelu(inner, approximate=True), pre_act)
    hidden = hidden.astype(jnp.bfloat16)
    grad_hidden = contract_cols(grad_branch_both, w_down)
    grad_pre = gelu_pullback(grad_hidden)[0].astype(jnp.bfloat16)
    grad_second = contract_cols(grad_pre, w_up)
    grad_second = grad_second[:local_rows] + to_half(
        grad_second[local_rows:].astype(jnp.bfloat16)
    ).astype(jnp.float32)
    grad_second = grad_second.reshape(FRAMES, frame_rows, D)
    _, second_pullback = jax.vjp(modulate, middle, shift_two, scale_two)
    middle_part, grad_shift_two, grad_scale_two = second_pullback(grad_second)
    grad_middle = upstream + middle_part
    grad_branch_one = (
        (gate_one[:, None, :] * grad_middle).astype(jnp.bfloat16).reshape(local_rows, D)
    )
    grad_gate_one = jnp.sum(grad_middle * branch_one, axis=1)
    grad_attended = contract_cols(grad_branch_one, w_out).astype(jnp.bfloat16)
    pieces = jnp.split(grad_attended, BANDS, axis=1)
    grad_attended = jnp.concatenate(
        [pieces[0], to_half(pieces[1]), to_pair(pieces[2]), to_both(pieces[3])]
    )

    branch_two = jnp.dot(hidden, w_down, preferred_element_type=jnp.float32)
    branch_two = branch_two[:local_rows] + to_half(
        branch_two[local_rows:].astype(jnp.bfloat16)
    ).astype(jnp.float32)
    branch_two = branch_two.reshape(FRAMES, frame_rows, D)
    activations = (
        (middle + gate_two[:, None, :] * branch_two).astype(jnp.bfloat16).reshape(1, local_rows, D)
    )
    grad_gate_two = jnp.sum(upstream * branch_two, axis=1)
    grad_down = contract_rows(hidden, grad_branch_both).astype(jnp.bfloat16)
    grad_up = contract_rows(second_both, grad_pre).astype(jnp.bfloat16)
    grad_out = contract_rows(attended, grad_branch_one)
    grad_out = relative_order(grad_out.reshape(BANDS, OWN_COLS, D), pair, half)
    grad_out = grad_out.reshape(groups, 2, own_rows, D)
    mine = jnp.where(half == 0, grad_out[:, 0], grad_out[:, 1])
    other = jnp.where(half == 0, grad_out[:, 1], grad_out[:, 0]).astype(jnp.bfloat16)
    grad_out = (mine + to_half(other).astype(jnp.float32)).astype(jnp.bfloat16)
    packed = jnp.concatenate(
        [
            grad_down.reshape(groups, down_rows, D),
            grad_up.reshape(groups, 2, own_rows, 2, D)
            .transpose(0, 1, 3, 2, 4)
            .reshape(groups, 4 * own_rows, D),
            grad_out,
        ],
        axis=1,
    )
    packed = lax.psum_scatter(
        packed.reshape(-1, D), ("clip", "pair"), scatter_dimension=0, tiled=True
    )
    early = band_sum(
        jnp.concatenate([grad_gate_one, grad_shift_two, grad_scale_two, grad_gate_two])
    )
    early = jnp.concatenate(
        [early, condition.astype(jnp.float32), jnp.zeros((4, D), jnp.float32)]
    )
    early = lax.all_gather(early, "clip")

    grad_projected = attend_back(frame_counts, projected, grad_attended, raw, local_rows)
    grad_projected, packed, early = lax.optimization_barrier((grad_projected, packed, early))
    grad_qkv = contract_rows(first_in, grad_projected).astype(jnp.bfloat16)
    grad_qkv = lax.psum_scatter(grad_qkv, "clip", scatter_dimension=0, tiled=True)
    grad_first = contract_cols(grad_projected, w_qkv)
    grad_first = grad_first.reshape(BANDS, FRAMES, frame_rows, D)
    late = jnp.concatenate(
        [jnp.sum(grad_first, axis=(0, 2)), jnp.sum(grad_first * normed, axis=(0, 2))]
    )
    late = clip_gather(band_sum(late), clip, clips).reshape(clips, 2 * FRAMES, D)
    low = grad_first.astype(jnp.bfloat16)
    own_part = grad_first[0] + to_half(low[1]).astype(jnp.float32)
    far_part = grad_first[2] + to_half(low[3]).astype(jnp.float32)
    grad_first = own_part + to_pair(far_part.astype(jnp.bfloat16)).astype(jnp.float32)
    _, first_pullback = jax.vjp(lambda inner: modulate(inner, shift_one, scale_one), residual)
    input_grad = (grad_middle + first_pullback(grad_first)[0]).reshape(1, local_rows, D)

    grad_qkv = grad_qkv.reshape(BANDS, own_rows, 3 * OWN_COLS)
    grad_qkv = lax.all_to_all(grad_qkv, ("pair", "half"), 0, 0)
    grad_qkv = grad_qkv.reshape(BANDS, own_rows, 3, OWN_COLS).transpose(1, 2, 0, 3)
    grad_qkv = grad_qkv.reshape(own_rows, 3 * D).astype(jnp.float32)
    grad_down = packed[:down_rows]
    grad_up = packed[down_rows : down_rows + 4 * own_rows].reshape(2, 2, own_rows, D)
    grad_out = packed[down_rows + 4 * own_rows :]
    mine = jnp.where(half == 0, grad_up[0], grad_up[1])
    other = to_half(jnp.where(half == 0, grad_up[1], grad_up[0]))

    def to_groups(tensor):
        tensor = tensor.transpose(1, 0, 2).reshape(own_rows, up_groups, LANES)
        return tensor

    grad_up = in_order(to_groups(mine), to_groups(other), half, axis=2)
    grad_up = grad_up.reshape(own_rows, FF).astype(jnp.float32)
    conditions = early[:, 4 * FRAMES : 5 * FRAMES].reshape(clips * FRAMES, D)
    grad_modulation = jnp.concatenate([late, early[:, : 4 * FRAMES]], axis=1)
    grad_modulation = grad_modulation.reshape(clips, 6, FRAMES, D)
    grad_modulation = grad_modulation.transpose(0, 2, 1, 3).reshape(clips * FRAMES, 6 * D)
    device = (clip * 2 + pair) * 2 + half
    grad_ada = contract_rows(
        lax.dynamic_slice_in_dim(conditions, device * own_rows, own_rows, axis=1),
        grad_modulation,
        precision=lax.Precision.HIGHEST,
    )
    reduced = (
        grad_qkv,
        grad_out.astype(jnp.float32),
        grad_up,
        grad_down.astype(jnp.float32),
        grad_ada,
    )
    local_squares = sum((jnp.sum(piece * piece) for piece in reduced))
    squares = sum_everywhere(jnp.full((8, LANES), local_squares), clips)
    grad_norm = jnp.sqrt(squares[0, 0])
    factor = jnp.minimum(1.0, clip_limit / (grad_norm + 1e-06))
    results = []
    for master, gradient, first, second in zip(masters, reduced, firsts, seconds):
        results.extend(adam_step(master, gradient * factor, first, second))
    return (activations, input_grad, grad_norm, *results)


def embed_levels(levels):
    halfway = D // 2
    spacing = jnp.exp(-math.log(10000.0) * jnp.arange(halfway, dtype=jnp.float32) / halfway)
    angles = levels.astype(jnp.float32)[..., None] * spacing
    return jax.nn.silu(jnp.concatenate([jnp.cos(angles), jnp.sin(angles)], axis=-1))


def solution(mesh):
    clips, bands = mesh.devices.shape
    split = Mesh(mesh.devices.reshape(clips, bands // 2, 2), ("clip", "pair", "half"))
    rows = P(("clip", "pair", "half"), None)
    activation = P("clip", ("pair", "half"), None)
    return jax.shard_map(
        per_device,
        mesh=split,
        in_specs=(activation, activation, P("clip"), P("clip", None)) + (rows,) * 15,
        out_specs=(activation, activation, P()) + (rows,) * 15,
        check_vma=False,
    )
```

```python
import math

import jax
import jax.numpy as jnp
from jax import lax
from jax.sharding import Mesh, PartitionSpec as P

D = 1024
HEADS = 16
HEAD_DIM = 64
FF = 4096
FRAMES = 12
STEP = 10
BANDS = 4
OWN_COLS = D // BANDS
LANES = 128

beta_first = 0.9
beta_second = 0.99
learn_rate = 0.03
weight_decay = 0.01
adam_epsilon = 1e-08
clip_limit = 1.0
norm_epsilon = 1e-06
masked_score = -1000000000.0


def contract_rows(left, right, precision=None):
    return lax.dot_general(
        left,
        right,
        (((0,), (0,)), ((), ())),
        precision=precision,
        preferred_element_type=jnp.float32,
    )


def contract_cols(left, right):
    return lax.dot_general(
        left, right, (((1,), (1,)), ((), ())), preferred_element_type=jnp.float32
    )


def normalize(values):
    average = jnp.mean(values, axis=-1, keepdims=True)
    centred = values - average
    variance = jnp.mean(centred * centred, axis=-1, keepdims=True)
    return centred * lax.rsqrt(variance + norm_epsilon)


def modulate(residual, shift, scale):
    return normalize(residual) * (1.0 + scale[:, None, :]) + shift[:, None, :]


def to_half(tensor):
    return lax.ppermute(tensor, "half", [(0, 1), (1, 0)])


def to_pair(tensor):
    return lax.ppermute(tensor, "pair", [(0, 1), (1, 0)])


def to_both(tensor):
    return lax.ppermute(tensor, ("pair", "half"), [(0, 3), (1, 2), (2, 1), (3, 0)])


def band_sum(tensor):
    tensor = tensor + to_half(tensor)
    return tensor + to_pair(tensor)


def clip_exchange(tensor, distance, clips):
    return lax.ppermute(tensor, "clip", [(place, place ^ distance) for place in range(clips)])


def clip_gather(tensor, clip, clips):
    distance = 1
    while distance < clips:
        other = clip_exchange(tensor, distance, clips)
        later = (clip // distance) % 2 == 1
        tensor = jnp.where(
            later, jnp.concatenate([other, tensor]), jnp.concatenate([tensor, other])
        )
        distance *= 2
    return tensor


def sum_everywhere(tensor, clips):
    tensor = band_sum(tensor)
    distance = 1
    while distance < clips:
        tensor = tensor + clip_exchange(tensor, distance, clips)
        distance *= 2
    return tensor


def in_order(own, other, index, axis=0):
    return jnp.where(
        index == 0, jnp.stack([own, other], axis=axis), jnp.stack([other, own], axis=axis)
    )


def relative_order(blocks, pair, half):
    rest = blocks.shape[1:]
    blocks = blocks.reshape((2, 2) + rest)
    blocks = jnp.where(half == 1, blocks[:, ::-1], blocks)
    blocks = jnp.where(pair == 1, blocks[::-1], blocks)
    return blocks.reshape((BANDS,) + rest)


def heads_of(tensor):
    return tensor.reshape(tensor.shape[0], -1, HEAD_DIM).transpose(1, 0, 2)


def columns_of(heads):
    return heads.transpose(1, 0, 2).reshape(heads.shape[1], -1)


def valid_keys(count, rows, local_rows):
    return jnp.arange(rows, dtype=jnp.int32) % local_rows // (local_rows // FRAMES) < count[0]


def with_mask(query, key, count, local_rows):
    rows = key.shape[1]
    bias = jnp.where(valid_keys(count, rows, local_rows), 0.0, masked_score).astype(jnp.bfloat16)
    bias = jnp.broadcast_to(bias[None, :, None], (key.shape[0], rows, 1))
    query = query * jnp.bfloat16(0.125)
    return (
        jnp.concatenate([query, jnp.ones_like(bias)], axis=2),
        jnp.concatenate([key, bias], axis=2),
    )


def attend(count, projected, local_rows):
    rows = projected.shape[0]
    heads = heads_of(projected).reshape(3, BANDS, rows, HEAD_DIM)

    def one_head(pieces):
        query, key, value = pieces

        def one_block(query_part):
            scores = contract_cols(query_part, key)
            maxima = jnp.max(scores, axis=1, keepdims=True)
            exponent = jnp.exp(scores - maxima).astype(jnp.bfloat16)
            outcome = jnp.dot(exponent, value, preferred_element_type=jnp.float32)
            totals = outcome[:, HEAD_DIM:]
            return outcome[:, :HEAD_DIM] / totals, (maxima + jnp.log(totals))[:, 0]

        parts = []
        for part in jnp.split(query, BANDS):
            if parts:
                part, parts[-1] = lax.optimization_barrier((part, parts[-1]))
            parts.append(one_block(part))
        return jnp.concatenate([part[0] for part in parts]), jnp.stack([part[1] for part in parts])

    query, key = with_mask(heads[0], heads[1], count, local_rows)
    value = jnp.concatenate([heads[2], jnp.ones_like(heads[2][:, :, :1])], axis=2)
    outcome, logs = lax.map(one_head, (query, key, value))
    return columns_of(outcome.astype(jnp.bfloat16)), (outcome, logs)


def attend_back(count, projected, grad_attended, raw, local_rows):
    rows = projected.shape[0]
    heads = heads_of(projected).reshape(3, BANDS, rows, HEAD_DIM)
    outcome, logs = raw
    grads = heads_of(grad_attended)
    deltas = jnp.sum(outcome * grads.astype(jnp.float32), axis=-1).reshape(logs.shape)

    def one_head(pieces):
        query, masked_query, key, masked_key, value, log_head, delta_head, grad = pieces

        def one_block(running, inputs):
            key_sum, value_sum = running
            query_part, masked_part, log_part, delta_part, grad_part = inputs
            scores = contract_cols(masked_part, masked_key)
            probability = jnp.exp(scores - log_part[:, None]).astype(jnp.bfloat16)
            probability = lax.optimization_barrier(probability)
            grad_prob = contract_cols(grad_part, value) - delta_part[:, None]
            grad_scores = (probability.astype(jnp.float32) * grad_prob).astype(jnp.bfloat16)
            grad_scores = lax.optimization_barrier(grad_scores)
            grad_query = jnp.dot(grad_scores, key, preferred_element_type=jnp.float32) * 0.125
            key_sum = key_sum + contract_rows(grad_scores, query_part) * 0.125
            value_sum = value_sum + contract_rows(probability, grad_part)
            return (key_sum, value_sum), grad_query.astype(jnp.bfloat16)

        running = (0.0, 0.0)
        grad_query = []
        for place in range(BANDS):
            part = slice(place * local_rows, (place + 1) * local_rows)
            running, grad_part = one_block(
                running,
                (query[part], masked_query[part], log_head[place], delta_head[place], grad[part]),
            )
            grad_query.append(grad_part)
        key_sum, value_sum = running
        return (
            jnp.concatenate(grad_query),
            key_sum.astype(jnp.bfloat16),
            value_sum.astype(jnp.bfloat16),
        )

    masked_query, masked_key = with_mask(heads[0], heads[1], count, local_rows)
    results = lax.map(
        one_head,
        (heads[0], masked_query, heads[1], masked_key, heads[2], logs, deltas, grads),
    )
    return jnp.concatenate([columns_of(result) for result in results], axis=1)


def adam_step(master, clipped, first, second):
    first_new = beta_first * first + (1.0 - beta_first) * clipped
    second_new = beta_second * second + (1.0 - beta_second) * clipped * clipped
    first_hat = first_new / (1.0 - beta_first**STEP)
    second_hat = second_new / (1.0 - beta_second**STEP)
    updated = master - learn_rate * (
        first_hat / (jnp.sqrt(second_hat) + adam_epsilon) + weight_decay * master
    )
    return (updated, first_new, second_new)


def per_device(
    tokens,
    cotangent,
    frame_counts,
    noise_levels,
    qkv_master,
    out_master,
    up_master,
    down_master,
    ada_master,
    qkv_first,
    out_first,
    up_first,
    down_first,
    ada_first,
    qkv_second,
    out_second,
    up_second,
    down_second,
    ada_second,
):
    clips = lax.axis_size("clip")
    clip, pair, half = lax.axis_index("clip"), lax.axis_index("pair"), lax.axis_index("half")
    everywhere = ("clip", "pair", "half")
    masters = (qkv_master, out_master, up_master, down_master, ada_master)
    firsts = (qkv_first, out_first, up_first, down_first, ada_first)
    seconds = (qkv_second, out_second, up_second, down_second, ada_second)
    local_rows = tokens.shape[1]
    frame_rows = local_rows // FRAMES
    own_rows = qkv_master.shape[0]
    up_groups = FF // (2 * LANES)

    own_tokens = tokens[0]
    half_tokens = to_half(own_tokens)
    pair_tokens = to_pair(own_tokens)
    clip_tokens = jnp.stack([own_tokens, half_tokens, pair_tokens, to_half(pair_tokens)])

    w_first = jnp.concatenate(
        [
            qkv_master.astype(jnp.bfloat16)
            .reshape(own_rows, 3, BANDS, OWN_COLS)
            .transpose(2, 0, 1, 3)
            .reshape(BANDS, own_rows, 3 * OWN_COLS),
            ada_master.astype(jnp.bfloat16)
            .reshape(own_rows, BANDS, 6 * OWN_COLS)
            .transpose(1, 0, 2),
        ],
        axis=2,
    )
    w_first = lax.all_to_all(w_first, ("pair", "half"), 0, 0)
    w_first = lax.all_gather(w_first.reshape(BANDS * own_rows, 9 * OWN_COLS), "clip", tiled=True)
    w_qkv = w_first[:, : 3 * OWN_COLS]

    condition = embed_levels(noise_levels[0]).astype(jnp.bfloat16)
    modulation = jnp.dot(condition, w_first[:, 3 * OWN_COLS :], preferred_element_type=jnp.float32)
    modulation = in_order(modulation, to_half(modulation), half)
    modulation = in_order(modulation, to_pair(modulation), pair)
    modulation = modulation.reshape(BANDS, FRAMES, 6 * OWN_COLS).transpose(1, 0, 2)
    shift_one, scale_one, gate_one, shift_two, scale_two, gate_two = jnp.split(
        modulation.reshape(FRAMES, 6 * D), 6, axis=1
    )

    groups = clips * (BANDS // 2)
    down_rows = down_master.shape[0]
    up_low = up_master.astype(jnp.bfloat16).reshape(own_rows, up_groups, 2, LANES)
    mine = jnp.where(half == 0, up_low[:, :, 0], up_low[:, :, 1]).reshape(own_rows, FF // 2)
    other = jnp.where(half == 0, up_low[:, :, 1], up_low[:, :, 0]).reshape(own_rows, FF // 2)
    up_low = in_order(mine, to_half(other), half).reshape(2, own_rows, 2, D)
    up_low = up_low.transpose(0, 2, 1, 3).reshape(4 * own_rows, D)
    w_rest = jnp.concatenate(
        [down_master.astype(jnp.bfloat16), up_low, out_master.astype(jnp.bfloat16)]
    )
    w_rest = lax.all_gather(w_rest, ("clip", "pair"))
    w_out = w_rest[:, down_rows + 4 * own_rows :]
    w_out = in_order(w_out, to_half(w_out), half, axis=1)
    w_out = relative_order(w_out.reshape(BANDS, OWN_COLS, D), pair, half).reshape(D, D)
    w_down = w_rest[:, :down_rows].reshape(FF // 2, D)
    w_up = w_rest[:, down_rows : down_rows + 4 * own_rows].reshape(groups, 2, 2, own_rows, D)
    w_up = w_up.transpose(0, 1, 3, 2, 4).reshape(D, FF // 2)

    wide = clip_tokens.astype(jnp.float32).reshape(BANDS, FRAMES, frame_rows, D)
    normed = normalize(wide)
    first_in = normed * (1.0 + scale_one[None, :, None, :]) + shift_one[None, :, None, :]
    first_in = first_in.astype(jnp.bfloat16).reshape(BANDS * local_rows, D)
    projected = jnp.dot(first_in, w_qkv, preferred_element_type=jnp.float32).astype(jnp.bfloat16)
    attended, raw = attend(frame_counts, projected, local_rows)
    attended = attended.reshape(BANDS, local_rows, OWN_COLS)
    attended = jnp.concatenate(
        [attended[0], to_half(attended[1]), to_pair(attended[2]), to_both(attended[3])], axis=1
    )

    residual = own_tokens.astype(jnp.float32).reshape(FRAMES, frame_rows, D)
    branch_one = jnp.dot(attended, w_out, preferred_element_type=jnp.float32).reshape(
        FRAMES, frame_rows, D
    )
    middle = residual + gate_one[:, None, :] * branch_one
    second_in = modulate(middle, shift_two, scale_two).astype(jnp.bfloat16).reshape(local_rows, D)
    upstream = cotangent[0].astype(jnp.float32).reshape(FRAMES, frame_rows, D)
    grad_branch_two = (gate_two[:, None, :] * upstream).astype(jnp.bfloat16).reshape(local_rows, D)
    second_both = jnp.concatenate([second_in, to_half(second_in)])
    grad_branch_both = jnp.concatenate([grad_branch_two, to_half(grad_branch_two)])

    pre_act = jnp.dot(second_both, w_up, preferred_element_type=jnp.float32)
    hidden, gelu_pullback = jax.vjp(lambda inner: jax.nn.gelu(inner, approximate=True), pre_act)
    hidden = hidden.astype(jnp.bfloat16)
    grad_hidden = contract_cols(grad_branch_both, w_down)
    grad_pre = gelu_pullback(grad_hidden)[0].astype(jnp.bfloat16)
    grad_second = contract_cols(grad_pre, w_up)
    grad_second = grad_second[:local_rows] + to_half(
        grad_second[local_rows:].astype(jnp.bfloat16)
    ).astype(jnp.float32)
    grad_second = grad_second.reshape(FRAMES, frame_rows, D)
    _, second_pullback = jax.vjp(modulate, middle, shift_two, scale_two)
    middle_part, grad_shift_two, grad_scale_two = second_pullback(grad_second)
    grad_middle = upstream + middle_part
    grad_branch_one = (
        (gate_one[:, None, :] * grad_middle).astype(jnp.bfloat16).reshape(local_rows, D)
    )
    grad_gate_one = jnp.sum(grad_middle * branch_one, axis=1)
    grad_attended = contract_cols(grad_branch_one, w_out).astype(jnp.bfloat16)
    pieces = jnp.split(grad_attended, BANDS, axis=1)
    grad_attended = jnp.concatenate(
        [pieces[0], to_half(pieces[1]), to_pair(pieces[2]), to_both(pieces[3])]
    )

    branch_two = jnp.dot(hidden, w_down, preferred_element_type=jnp.float32)
    branch_two = branch_two[:local_rows] + to_half(
        branch_two[local_rows:].astype(jnp.bfloat16)
    ).astype(jnp.float32)
    branch_two = branch_two.reshape(FRAMES, frame_rows, D)
    activations = (
        (middle + gate_two[:, None, :] * branch_two).astype(jnp.bfloat16).reshape(1, local_rows, D)
    )
    grad_gate_two = jnp.sum(upstream * branch_two, axis=1)
    grad_down = contract_rows(hidden, grad_branch_both).astype(jnp.bfloat16)
    grad_up = contract_rows(second_both, grad_pre).astype(jnp.bfloat16)
    grad_out = contract_rows(attended, grad_branch_one)
    grad_out = relative_order(grad_out.reshape(BANDS, OWN_COLS, D), pair, half)
    grad_out = grad_out.reshape(groups, 2, own_rows, D)
    mine = jnp.where(half == 0, grad_out[:, 0], grad_out[:, 1])
    other = jnp.where(half == 0, grad_out[:, 1], grad_out[:, 0]).astype(jnp.bfloat16)
    grad_out = (mine + to_half(other).astype(jnp.float32)).astype(jnp.bfloat16)
    packed = jnp.concatenate(
        [
            grad_down.reshape(groups, down_rows, D),
            grad_up.reshape(groups, 2, own_rows, 2, D)
            .transpose(0, 1, 3, 2, 4)
            .reshape(groups, 4 * own_rows, D),
            grad_out,
        ],
        axis=1,
    )
    packed = lax.psum_scatter(
        packed.reshape(-1, D), ("clip", "pair"), scatter_dimension=0, tiled=True
    )
    early = band_sum(
        jnp.concatenate([grad_gate_one, grad_shift_two, grad_scale_two, grad_gate_two])
    )
    early = jnp.concatenate(
        [early, condition.astype(jnp.float32), jnp.zeros((4, D), jnp.float32)]
    )
    early = lax.all_gather(early, "clip")

    grad_projected = attend_back(frame_counts, projected, grad_attended, raw, local_rows)
    grad_projected, packed, early = lax.optimization_barrier((grad_projected, packed, early))
    grad_qkv = contract_rows(first_in, grad_projected).astype(jnp.bfloat16)
    grad_qkv = lax.psum_scatter(grad_qkv, "clip", scatter_dimension=0, tiled=True)
    grad_first = contract_cols(grad_projected, w_qkv)
    grad_first = grad_first.reshape(BANDS, FRAMES, frame_rows, D)
    late = jnp.concatenate(
        [jnp.sum(grad_first, axis=(0, 2)), jnp.sum(grad_first * normed, axis=(0, 2))]
    )
    late = clip_gather(band_sum(late), clip, clips).reshape(clips, 2 * FRAMES, D)
    low = grad_first.astype(jnp.bfloat16)
    own_part = grad_first[0] + to_half(low[1]).astype(jnp.float32)
    far_part = grad_first[2] + to_half(low[3]).astype(jnp.float32)
    grad_first = own_part + to_pair(far_part.astype(jnp.bfloat16)).astype(jnp.float32)
    _, first_pullback = jax.vjp(lambda inner: modulate(inner, shift_one, scale_one), residual)
    input_grad = (grad_middle + first_pullback(grad_first)[0]).reshape(1, local_rows, D)

    grad_qkv = grad_qkv.reshape(BANDS, own_rows, 3 * OWN_COLS)
    grad_qkv = lax.all_to_all(grad_qkv, ("pair", "half"), 0, 0)
    grad_qkv = grad_qkv.reshape(BANDS, own_rows, 3, OWN_COLS).transpose(1, 2, 0, 3)
    grad_qkv = grad_qkv.reshape(own_rows, 3 * D).astype(jnp.float32)
    grad_down = packed[:down_rows]
    grad_up = packed[down_rows : down_rows + 4 * own_rows].reshape(2, 2, own_rows, D)
    grad_out = packed[down_rows + 4 * own_rows :]
    mine = jnp.where(half == 0, grad_up[0], grad_up[1])
    other = to_half(jnp.where(half == 0, grad_up[1], grad_up[0]))

    def to_groups(tensor):
        tensor = tensor.transpose(1, 0, 2).reshape(own_rows, up_groups, LANES)
        return tensor

    grad_up = in_order(to_groups(mine), to_groups(other), half, axis=2)
    grad_up = grad_up.reshape(own_rows, FF).astype(jnp.float32)
    conditions = early[:, 4 * FRAMES : 5 * FRAMES].reshape(clips * FRAMES, D)
    grad_modulation = jnp.concatenate([late, early[:, : 4 * FRAMES]], axis=1)
    grad_modulation = grad_modulation.reshape(clips, 6, FRAMES, D)
    grad_modulation = grad_modulation.transpose(0, 2, 1, 3).reshape(clips * FRAMES, 6 * D)
    device = (clip * 2 + pair) * 2 + half
    grad_ada = contract_rows(
        lax.dynamic_slice_in_dim(conditions, device * own_rows, own_rows, axis=1),
        grad_modulation,
        precision=lax.Precision.HIGHEST,
    )
    reduced = (
        grad_qkv,
        grad_out.astype(jnp.float32),
        grad_up,
        grad_down.astype(jnp.float32),
        grad_ada,
    )
    local_squares = sum((jnp.sum(piece * piece) for piece in reduced))
    squares = sum_everywhere(jnp.full((8, LANES), local_squares), clips)
    grad_norm = jnp.sqrt(squares[0, 0])
    factor = jnp.minimum(1.0, clip_limit / (grad_norm + 1e-06))
    results = []
    for master, gradient, first, second in zip(masters, reduced, firsts, seconds):
        results.extend(adam_step(master, gradient * factor, first, second))
    return (activations, input_grad, grad_norm, *results)


def embed_levels(levels):
    halfway = D // 2
    spacing = jnp.exp(-math.log(10000.0) * jnp.arange(halfway, dtype=jnp.float32) / halfway)
    angles = levels.astype(jnp.float32)[..., None] * spacing
    return jax.nn.silu(jnp.concatenate([jnp.cos(angles), jnp.sin(angles)], axis=-1))


def solution(mesh):
    clips, bands = mesh.devices.shape
    split = Mesh(mesh.devices.reshape(clips, bands // 2, 2), ("clip", "pair", "half"))
    rows = P(("clip", "pair", "half"), None)
    activation = P("clip", ("pair", "half"), None)
    return jax.shard_map(
        per_device,
        mesh=split,
        in_specs=(activation, activation, P("clip"), P("clip", None)) + (rows,) * 15,
        out_specs=(activation, activation, P()) + (rows,) * 15,
        check_vma=False,
    )
```
